768 devices in a mesh: row: 32 (over y, x), col: 24 (over z, core).
Axes of the slice: x: 4, y: 8, z: 12, core: 2. Of those that a mesh axis runs over, the one named last changes fastest.
Arguments:
- features: float32 [131072, 768], P('row', 'col'), may hold values from -6 to 6
- dest_feat: float32 [1536, 768], P('row', 'col'), may hold values from -6 to 6
- owner: int32 [38400, 1], P('row'), may hold values from 0 to 31; in each aligned block of 1200 rows (0 to 1199, 1200 to 2399, ...) at most 75 rows name the same one
- local_row: int32 [38400], P('row'), may hold values from 0 to 4095
- w_self: float32 [768, 1024], P('col'), may hold values from -0.21875 to 0.21875
- w_neigh: float32 [768, 1024], P('col'), may hold values from -0.4375 to 0.4375
- grad_out: float32 [1536, 1024], P('row'), may hold values from -6 to 6
Outputs:
- hidden: float32 [1536, 1024], P('row')
- grad_self: float32 [768, 1024], P('col')
- grad_neigh: float32 [768, 1024], P('col')
The draws below stay inside these ranges and needn't reach their ends.
Inputs may be any that keep to these rules, and one draw needn't show every extreme that they name: Among the samples of one index of row, at most 75 have the same owner, and some owner has exactly 75.
All inputs are finite; a program needn't handle non-finite values.
Results may differ from the reference program's by a relative error of at most 0.00008.
Values sent between devices are 32-bit elements; how exact they have to be, the bound alone decides.
No kernel may reach another device: no remote copies, remote signals or barrier semaphores. Data moves between devices by JAX's collectives and lax.ppermute only.
A program may use at most 32 MiB of HBM per device.

```python
import math
import jax
import jax.numpy as jnp
import numpy as np
from jax import lax

F = 768
HID = 1024
FAN = 25
DST_DEV = 48
NODES_DEV = 4096
CAP = 75
DST_TOT = 1536
SAMPLES = 38400
NODES = 131072
N_ROW = 32


def set_ends(result, own_key, least, high):
    spot = [jax.random.randint(jax.random.fold_in(own_key, axis), (), 0, length) for axis, length in enumerate(result.shape)]
    main_axis = result.shape.index(max(result.shape))
    next_to = spot[:main_axis] + [(spot[main_axis] + 1) % result.shape[main_axis]] + spot[main_axis + 1:]
    return result.at[tuple(spot)].set(least).at[tuple(next_to)].set(high)


def steps_of(key, dims, shards, smallest, high):
    level = 1.0
    for axis_at, shards_of in shards:
        steps = jax.random.uniform(jax.random.fold_in(jax.random.fold_in(key, 6), axis_at), (shards_of,), jnp.float32, smallest / len(shards), high / len(shards))
        level = level * jnp.repeat(jnp.exp(steps), dims[axis_at] // shards_of).reshape((-1,) + (1,) * (len(dims) - 1 - axis_at))
    return level


def routed_block(rng, own, number, rows, number_of, top, limit, lean):
    ranking = jax.random.permutation(rng, number_of)
    heavy_load, ordinary = portions_of(number_of, rows * top, limit, lean, True), portions_of(number_of, rows * top, limit, lean, False)
    places = jnp.arange(number_of)

    def named(tallies, offset_by):
        used = int((tallies > 0).sum())
        fixed = max(1, used // 4)
        shifted = fixed + (places - fixed + offset_by * (used - fixed)) % max(1, number_of - fixed)
        return jnp.zeros((number_of,), jnp.int32).at[ranking[jnp.where(places < fixed, places, shifted)]].set(jnp.asarray(tallies, jnp.int32))

    tallies = jnp.where(number % 4 == 0, named(heavy_load, number // 4), named(ordinary, number - number // 4 - 1))
    mixed = jax.random.permutation(jax.random.fold_in(own, 3), number_of)
    donor, sink = mixed[0:number_of // 2 * 2:2], mixed[1:number_of // 2 * 2:2]
    slack = jnp.minimum(tallies[donor] - 1, limit - tallies[sink]) // 2
    slack = jnp.where((donor == ranking[0]) | (sink == ranking[0]) | (tallies[sink] == 0), 0, jnp.maximum(slack, 0))
    shifted = jax.random.randint(jax.random.fold_in(own, 4), (number_of // 2,), 0, 1 << 20) % (slack + 1)
    tallies = tallies.at[donor].add(-shifted).at[sink].add(shifted)
    items = jnp.searchsorted(jnp.cumsum(tallies), jnp.arange(rows * top), side="right").astype(jnp.int32)
    grid = items.reshape(top, rows).T
    grid = grid[jax.random.permutation(jax.random.fold_in(own, 1), rows)]
    offset_by = jax.random.randint(jax.random.fold_in(own, 2), (rows, 1), 0, top)
    return jnp.take_along_axis(grid, (jnp.arange(top)[None, :] + offset_by) % top, axis=1)


def portions_of(count, total, reach, skew, full):
    portions = [(1 << 20) // math.isqrt(grade ** skew) + 1 for grade in range(1, count + 1)]
    largest = reach if full else min(reach, max(-(-total // count), total * portions[0] // sum(portions)))
    least = 1 if total - largest >= count - 1 else 0
    holding, spare = [largest] + [least] * (count - 1), total - largest - least * (count - 1)
    while spare > 0:
        candidates = [i for i in range(1, count) if holding[i] < largest] or [i for i in range(1, count) if holding[i] < reach]
        mass, remaining = sum([portions[i] for i in candidates]), spare
        for i in candidates:
            extra = min(reach - holding[i], max(1, remaining * portions[i] // mass), spare)
            holding[i] = holding[i] + extra
            spare = spare - extra
    return np.array(holding)


def gaussian(rng, shape, deviation, most, shards=(), dtype=jnp.bfloat16):
    result = deviation * jax.random.normal(rng, shape, jnp.float32)
    if shards:
        result = result * steps_of(rng, shape, shards, -0.22, 0.18)
    return jnp.clip(result, -most, most).astype(dtype)


def setup_inputs(seed: int = 0) -> dict:
    key_list = jax.random.split(jax.random.key(seed), 8)
    features = gaussian(key_list[0], (NODES, F), 1.0, 6.0, ((0, 32), (1, 24)), jnp.float32)
    dest_feat = gaussian(key_list[1], (DST_TOT, F), 1.0, 6.0, ((0, 32), (1, 24)), jnp.float32)
    owner_keys = jax.random.split(jax.random.fold_in(key_list[2], 1), SAMPLES // (DST_DEV * FAN))
    owner_turns = jax.random.permutation(jax.random.fold_in(key_list[2], 3), SAMPLES // (DST_DEV * FAN))
    owner = jax.vmap(lambda own, number: routed_block(jax.random.fold_in(key_list[2], 2), own, number, DST_DEV * FAN, N_ROW, 1, CAP, 2))(owner_keys, owner_turns).reshape((SAMPLES, 1))
    local_row = set_ends(jax.random.randint(key_list[3], (SAMPLES,), 0, NODES_DEV), jax.random.fold_in(key_list[3], 1), 0, NODES_DEV - 1).astype(jnp.int32)
    w_self = gaussian(key_list[4], (F, HID), F ** -0.5, 0.21875, ((0, 24),), jnp.float32)
    w_neigh = gaussian(key_list[5], (F, HID), (F // 4) ** -0.5, 0.4375, ((0, 24),), jnp.float32)
    grad_out = gaussian(key_list[6], (DST_TOT, HID), 1.0, 6.0, ((0, 32),), jnp.float32)
    return dict(features=features, dest_feat=dest_feat, owner=owner, local_row=local_row, w_self=w_self, w_neigh=w_neigh, grad_out=grad_out)


def gelu_tanh(value):
    return jax.nn.gelu(value, approximate=True)

def reference(features, dest_feat, owner, local_row, w_self, w_neigh, grad_out):
    node_ids = (owner[:, 0] * NODES_DEV + local_row).astype(jnp.int32)
    picked = jnp.take(features, node_ids, axis=0)
    agg = lax.optimization_barrier(jnp.sum(picked.reshape(DST_TOT, FAN, F), axis=1)) / FAN
    pre = jnp.dot(dest_feat, w_self, precision=lax.Precision.HIGHEST, preferred_element_type=jnp.float32)
    pre = pre + jnp.dot(agg, w_neigh, precision=lax.Precision.HIGHEST, preferred_element_type=jnp.float32)
    hidden, back_fn = jax.vjp(gelu_tanh, pre)
    slope = back_fn(jnp.ones_like(pre))[0]
    dpre = grad_out * slope
    grad_self = jnp.dot(dest_feat.T, dpre, precision=lax.Precision.HIGHEST, preferred_element_type=jnp.float32)
    grad_neigh = jnp.dot(agg.T, dpre, precision=lax.Precision.HIGHEST, preferred_element_type=jnp.float32)
    return (hidden, grad_self, grad_neigh)
```

```python
import jax
import jax.numpy as jnp
from jax import lax
from jax.sharding import Mesh, PartitionSpec as P

FAN = 25
DST = 48
SLOTS = 128
ROW = ("y", "x")
COL = ("z", "core")
N_ROW = 32
N_Z = 12
HIGH = lax.Precision.HIGH
HIGHEST = lax.Precision.HIGHEST


def gelu_tanh(value):
    return jax.nn.gelu(value, approximate=True)


def activate(pre):
    hidden, back_fn = jax.vjp(gelu_tanh, pre)
    return (hidden, back_fn(jnp.ones_like(pre))[0])


def exchange(value, axis):
    return lax.all_to_all(value, axis, split_axis=0, concat_axis=0, tiled=True)


def slot_ranks(owners, owner_count):
    samples = owners.shape[0]
    block = 8 * FAN
    blocks = samples // block
    marks = (owners[:, None] == jnp.arange(owner_count, dtype=jnp.int32)[None, :]).astype(jnp.float32)
    marks = marks.reshape(blocks, block, owner_count)
    lower = (
        jnp.arange(block, dtype=jnp.int32)[:, None] >= jnp.arange(block, dtype=jnp.int32)[None, :]
    ).astype(jnp.float32)
    within = jnp.einsum("ij,bjo->bio", lower, marks, precision=HIGHEST)
    totals = within[:, block - 1, :]
    offsets = jnp.cumsum(totals, axis=0) - totals
    counted = within + offsets[:, None, :]
    rank = jnp.sum((counted - 1.0) * marks, axis=2).reshape(samples)
    return rank.astype(jnp.int32)


def requests(owners, local_row):
    rank = slot_ranks(owners, N_ROW)
    dest = jnp.arange(owners.shape[0], dtype=jnp.int32) // FAN + 1
    named = (owners[None, :] == jnp.arange(N_ROW, dtype=jnp.int32)[:, None]).astype(jnp.float32)
    slot = (rank[:, None] == jnp.arange(SLOTS, dtype=jnp.int32)[None, :]).astype(jnp.float32)
    both = jnp.stack([local_row, dest]).astype(jnp.float32)
    packed = (named[:, None, :] * both[None, :, :]).reshape(2 * N_ROW, owners.shape[0])
    return jnp.dot(packed, slot, precision=HIGHEST).astype(jnp.int32).reshape(N_ROW, 2, SLOTS)


def body(features, dest_feat, owner, local_row, w_self, w_neigh, grad_out):
    width = features.shape[1]
    hid = w_self.shape[1]
    own = dest_feat.T
    tail = jnp.pad(own, ((0, 0), (0, 128 - DST))).reshape(4, 8, 128).transpose(1, 0, 2).reshape(8, 512)
    tail = jnp.pad(tail, ((0, 0), (0, hid - 512)))
    gathered = lax.all_gather(jnp.concatenate([w_self, w_neigh, tail], axis=0), "z", axis=0, tiled=False)

    asked = exchange(requests(owner[:, 0], local_row), ROW)
    rows = jnp.take(features, asked[:, 0, :75], axis=0)
    placed = (
        asked[:, 1, None, :75] == jnp.arange(1, DST + 1, dtype=jnp.int32)[None, :, None]
    ).astype(jnp.float32)
    part = jnp.einsum("rds,rsf->rfd", placed, rows, precision=HIGH)
    part = exchange(part.reshape(N_ROW, 12, 128), ROW)
    agg = jnp.sum(part, axis=0) / FAN
    others = exchange(jnp.broadcast_to(agg[None], (N_Z, 12, 128)), "z").reshape(N_Z * width, DST)
    agg = agg.reshape(width, DST)

    dests = gathered[:, 64:72, :512].reshape(N_Z, 8, 4, 128).transpose(0, 2, 1, 3).reshape(N_Z * width, 128)[:, :DST]
    pre = lax.dot_general(
        dests, gathered[:, :32].reshape(N_Z * width, hid), (((0,), (0,)), ((), ())), precision=HIGH
    )
    pre = pre + lax.dot_general(
        others, gathered[:, 32:64].reshape(N_Z * width, hid), (((0,), (0,)), ((), ())), precision=HIGH
    )
    pre = jnp.sum(lax.all_gather(pre, "core", axis=0, tiled=False), axis=0)
    hidden, slope = activate(pre)
    dpre = grad_out * slope
    part = jnp.dot(jnp.concatenate([own, agg], axis=0), dpre, precision=HIGH)
    part = part.reshape(4, 16, 8, 128).transpose(0, 2, 1, 3).reshape(N_ROW, 16, 128)
    total = jnp.sum(exchange(part, ROW), axis=0)
    grads = exchange(jnp.broadcast_to(total[None], (N_ROW, 16, 128)), ROW)
    grads = grads.reshape(4, 8, 16, 128).transpose(0, 2, 1, 3).reshape(64, hid)
    return (hidden, grads[:32], grads[32:])


def solution(mesh):
    grid = Mesh(mesh.devices.reshape(8, 4, 12, 2), ("y", "x", "z", "core"))
    return jax.shard_map(
        body,
        mesh=grid,
        in_specs=(P(ROW, COL), P(ROW, COL), P(ROW, None), P(ROW), P(COL, None), P(COL, None), P(ROW, None)),
        out_specs=(P(ROW, None), P(COL, None), P(COL, None)),
        check_vma=False,
    )
```

```python
import jax
import jax.numpy as jnp
from jax import lax
from jax.sharding import Mesh, PartitionSpec as P

FAN = 25
DST = 48
SLOTS = 128
ROW = ("y", "x")
COL = ("z", "core")
N_ROW = 32
N_Z = 12
HIGH = lax.Precision.HIGH
HIGHEST = lax.Precision.HIGHEST


def gelu_tanh(value):
    return jax.nn.gelu(value, approximate=True)


def activate(pre):
    hidden, back_fn = jax.vjp(gelu_tanh, pre)
    return (hidden, back_fn(jnp.ones_like(pre))[0])


def exchange(value, axis):
    return lax.all_to_all(value, axis, split_axis=0, concat_axis=0, tiled=True)


def slot_ranks(owners, owner_count):
    samples = owners.shape[0]
    block = 8 * FAN
    blocks = samples // block
    marks = (owners[:, None] == jnp.arange(owner_count, dtype=jnp.int32)[None, :]).astype(jnp.float32)
    marks = marks.reshape(blocks, block, owner_count)
    lower = (
        jnp.arange(block, dtype=jnp.int32)[:, None] >= jnp.arange(block, dtype=jnp.int32)[None, :]
    ).astype(jnp.float32)
    within = jnp.einsum("ij,bjo->bio", lower, marks, precision=HIGHEST)
    totals = within[:, block - 1, :]
    offsets = jnp.cumsum(totals, axis=0) - totals
    counted = within + offsets[:, None, :]
    rank = jnp.sum((counted - 1.0) * marks, axis=2).reshape(samples)
    return rank.astype(jnp.int32)


def requests(owners, local_row):
    rank = slot_ranks(owners, N_ROW)
    dest = jnp.arange(owners.shape[0], dtype=jnp.int32) // FAN + 1
    named = (owners[None, :] == jnp.arange(N_ROW, dtype=jnp.int32)[:, None]).astype(jnp.float32)
    slot = (rank[:, None] == jnp.arange(SLOTS, dtype=jnp.int32)[None, :]).astype(jnp.float32)
    both = jnp.stack([local_row, dest]).astype(jnp.float32)
    packed = (named[:, None, :] * both[None, :, :]).reshape(2 * N_ROW, owners.shape[0])
    return jnp.dot(packed, slot, precision=HIGHEST).astype(jnp.int32).reshape(N_ROW, 2, SLOTS)


def body(features, dest_feat, owner, local_row, w_self, w_neigh, grad_out):
    width = features.shape[1]
    hid = w_self.shape[1]
    own = dest_feat.T
    weights = lax.all_gather(jnp.concatenate([w_self, w_neigh], axis=0), "z", axis=0, tiled=True)

    asked = exchange(requests(owner[:, 0], local_row), ROW)
    rows = jnp.take(features, asked[:, 0, :75], axis=0)
    placed = (
        asked[:, 1, None, :75] == jnp.arange(1, DST + 1, dtype=jnp.int32)[None, :, None]
    ).astype(jnp.float32)
    part = jnp.einsum("rds,rsf->rfd", placed, rows, precision=HIGH)
    part = exchange(part.reshape(N_ROW, 12, 128), ROW)
    agg = (jnp.sum(part, axis=0) / FAN).reshape(width, DST)
    both = jnp.concatenate([own, agg], axis=0)
    sent = jnp.broadcast_to(both.reshape(1, 24, 128), (N_Z, 24, 128))
    others = exchange(sent, "z").reshape(N_Z * 2 * width, DST)
    pre = lax.dot_general(others, weights, (((0,), (0,)), ((), ())), precision=HIGH)
    pre = jnp.sum(lax.all_gather(pre, "core", axis=0, tiled=False), axis=0)
    hidden, slope = activate(pre)
    dpre = grad_out * slope
    part = jnp.dot(both, dpre, precision=HIGH)
    part = part.reshape(4, 16, 8, 128).transpose(0, 2, 1, 3).reshape(N_ROW, 16, 128)
    total = jnp.sum(exchange(part, ROW), axis=0)
    grads = exchange(jnp.broadcast_to(total[None], (N_ROW, 16, 128)), ROW)
    grads = grads.reshape(4, 8, 16, 128).transpose(0, 2, 1, 3).reshape(64, hid)
    return (hidden, grads[:32], grads[32:])


def solution(mesh):
    grid = Mesh(mesh.devices.reshape(8, 4, 12, 2), ("y", "x", "z", "core"))
    return jax.shard_map(
        body,
        mesh=grid,
        in_specs=(P(ROW, COL), P(ROW, COL), P(ROW, None), P(ROW), P(COL, None), P(COL, None), P(ROW, None)),
        out_specs=(P(ROW, None), P(COL, None), P(COL, None)),
        check_vma=False,
    )
```

```python
import jax
import jax.numpy as jnp
from jax import lax
from jax.sharding import Mesh, PartitionSpec as P

FAN = 25
DST = 48
SLOTS = 128
ROW = ("y", "x")
COL = ("z", "core")
N_ROW = 32
N_Z = 12
HIGH = lax.Precision.HIGH
HIGHEST = lax.Precision.HIGHEST


def gelu_tanh(value):
    return jax.nn.gelu(value, approximate=True)


def activate(pre):
    hidden, back_fn = jax.vjp(gelu_tanh, pre)
    return (hidden, back_fn(jnp.ones_like(pre))[0])


def exchange(value, axis):
    return lax.all_to_all(value, axis, split_axis=0, concat_axis=0, tiled=True)


def slot_ranks(owners, owner_count):
    samples = owners.shape[0]
    block = 8 * FAN
    blocks = samples // block
    marks = (owners[:, None] == jnp.arange(owner_count, dtype=jnp.int32)[None, :]).astype(jnp.float32)
    marks = marks.reshape(blocks, block, owner_count)
    lower = (
        jnp.arange(block, dtype=jnp.int32)[:, None] >= jnp.arange(block, dtype=jnp.int32)[None, :]
    ).astype(jnp.float32)
    within = jnp.einsum("ij,bjo->bio", lower, marks, precision=HIGHEST)
    totals = within[:, block - 1, :]
    offsets = jnp.cumsum(totals, axis=0) - totals
    counted = within + offsets[:, None, :]
    rank = jnp.sum((counted - 1.0) * marks, axis=2).reshape(samples)
    return rank.astype(jnp.int32)


def requests(owners, local_row):
    rank = slot_ranks(owners, N_ROW)
    dest = jnp.arange(owners.shape[0], dtype=jnp.int32) // FAN + 1
    named = (owners[None, :] == jnp.arange(N_ROW, dtype=jnp.int32)[:, None]).astype(jnp.float32)
    slot = (rank[:, None] == jnp.arange(SLOTS, dtype=jnp.int32)[None, :]).astype(jnp.float32)
    both = jnp.stack([local_row, dest]).astype(jnp.float32)
    packed = (named[:, None, :] * both[None, :, :]).reshape(2 * N_ROW, owners.shape[0])
    return jnp.dot(packed, slot, precision=HIGHEST).astype(jnp.int32).reshape(N_ROW, 2, SLOTS)


def body(features, dest_feat, owner, local_row, w_self, w_neigh, grad_out):
    width = features.shape[1]
    hid = w_self.shape[1]
    own = dest_feat.T

    asked = exchange(requests(owner[:, 0], local_row), ROW)
    rows = jnp.take(features, asked[:, 0, :75], axis=0)
    placed = (
        asked[:, 1, None, :75] == jnp.arange(1, DST + 1, dtype=jnp.int32)[None, :, None]
    ).astype(jnp.float32)
    part = jnp.einsum("rds,rsf->rfd", placed, rows, precision=HIGH)
    part = exchange(part.reshape(N_ROW, 12, 128), ROW)
    agg = (jnp.sum(part, axis=0) / FAN).reshape(width, DST)
    both = jnp.concatenate([own, agg], axis=0)
    pre = jnp.dot(dest_feat, w_self, precision=HIGH)
    pre = pre + lax.dot_general(agg, w_neigh, (((0,), (0,)), ((), ())), precision=HIGH)
    pair = lax.all_gather(pre.reshape(2, DST // 2, hid), "core", axis=0, tiled=False)
    half = jnp.sum(lax.dynamic_index_in_dim(pair, lax.axis_index("core"), axis=1, keepdims=False), axis=0)
    half = half.reshape(3, 8, 4, 256).transpose(0, 2, 1, 3).reshape(N_Z, 8, 256)
    tile = jnp.sum(exchange(half, "z"), axis=0)
    half = exchange(jnp.broadcast_to(tile[None], (N_Z, 8, 256)), "z")
    half = half.reshape(3, 4, 8, 256).transpose(0, 2, 1, 3).reshape(DST // 2, hid)
    pre = lax.all_gather(half, "core", axis=0, tiled=True)
    hidden, slope = activate(pre)
    dpre = grad_out * slope
    part = jnp.dot(both, dpre, precision=HIGH)
    part = part.reshape(4, 16, 8, 128).transpose(0, 2, 1, 3).reshape(N_ROW, 16, 128)
    total = jnp.sum(exchange(part, ROW), axis=0)
    grads = exchange(jnp.broadcast_to(total[None], (N_ROW, 16, 128)), ROW)
    grads = grads.reshape(4, 8, 16, 128).transpose(0, 2, 1, 3).reshape(64, hid)
    return (hidden, grads[:32], grads[32:])


def solution(mesh):
    grid = Mesh(mesh.devices.reshape(8, 4, 12, 2), ("y", "x", "z", "core"))
    return jax.shard_map(
        body,
        mesh=grid,
        in_specs=(P(ROW, COL), P(ROW, COL), P(ROW, None), P(ROW), P(COL, None), P(COL, None), P(ROW, None)),
        out_specs=(P(ROW, None), P(COL, None), P(COL, None)),
        check_vma=False,
    )
```

```python
import jax
import jax.numpy as jnp
from jax import lax
from jax.experimental import pallas as pl
from jax.experimental.pallas import tpu as pltpu
from jax.sharding import Mesh, PartitionSpec as P

FAN = 25
DST = 48
CAP = 75
ROOM = 80
SLOTS = 128
ROW = ("y", "x")
COL = ("z", "core")
N_ROW = 32
N_Z = 12
HIGH = lax.Precision.HIGH
LANES = (((1,), (1,)), ((), ()))
VMEM = pl.BlockSpec(memory_space=pltpu.VMEM)
SMEM = pl.BlockSpec(memory_space=pltpu.SMEM)
SMALL = pltpu.CompilerParams(vmem_limit_bytes=16 << 20)


def gelu_tanh(value):
    return jax.nn.gelu(value, approximate=True)


def activate(pre):
    hidden, back_fn = jax.vjp(gelu_tanh, pre)
    return (hidden, back_fn(jnp.ones_like(pre))[0])


def exchange(value, axis):
    return lax.all_to_all(value, axis, split_axis=0, concat_axis=0, tiled=True)


def request_kernel(owner_ref, row_ref, out_ref):
    samples = owner_ref.shape[1]
    blocks = -(-samples // 128)
    line = lax.broadcasted_iota(jnp.int32, (2 * N_ROW, 128), 0)
    lane = lax.broadcasted_iota(jnp.int32, (1, 128), 1)
    even = (line & 1) == 0
    before = lax.broadcasted_iota(jnp.int32, (128, 128), 0) >= lax.broadcasted_iota(jnp.int32, (128, 128), 1)
    before = jnp.where(before, 1.0, 0.0).astype(jnp.bfloat16)
    slot = lax.broadcasted_iota(jnp.int32, (SLOTS, 128), 0).astype(jnp.float32)

    def part(ref, block, fill):
        width = min(128, samples - block * 128)
        values = ref[:, block * 128 : block * 128 + width]
        if width < 128:
            values = jnp.concatenate([values, jnp.full((1, 128 - width), fill, jnp.int32)], axis=1)
        return values

    marks, counts = [], []
    for block in range(blocks):
        mark = part(owner_ref, block, -1) == (line >> 1)
        marks.append(mark)
        counts.append(
            lax.dot_general(
                jnp.where(mark, 1.0, 0.0).astype(jnp.bfloat16), before, LANES, preferred_element_type=jnp.float32
            )
        )
    seen = jnp.full((2 * N_ROW, 1), -1.0, jnp.float32)
    lefts, rights = [], []
    for block in range(blocks):
        rows = part(row_ref, block, 0)
        mark, count = marks[block], counts[block]
        rank = jnp.sum(jnp.where(mark & even, count + seen, 0.0), axis=0, keepdims=True)
        seen = seen + count[:, 127:128]
        rights.append(jnp.where(rank == slot, 1.0, 0.0).astype(jnp.bfloat16))
        dest = (lane + block * 128) // FAN + 1
        high = jnp.where(mark, jnp.where(even, rows >> 6, dest), 0).astype(jnp.float32)
        low = jnp.where(mark & even, rows & 63, 0).astype(jnp.float32)
        lefts.append(jnp.concatenate([high, low], axis=0).astype(jnp.bfloat16))
    total = lax.dot_general(
        jnp.concatenate(lefts, axis=1), jnp.concatenate(rights, axis=1), LANES, preferred_element_type=jnp.float32
    )
    first, second = total[: 2 * N_ROW], total[2 * N_ROW :]
    out_ref[...] = (jnp.where(even, first * 64.0, first) + second).astype(jnp.int32)


def requests(owner, local_row):
    return pl.pallas_call(
        request_kernel,
        in_specs=[VMEM, VMEM],
        out_specs=VMEM,
        out_shape=jax.ShapeDtypeStruct((2 * N_ROW, SLOTS), jnp.int32),
        compiler_params=SMALL,
        name="requests",
    )(owner, local_row)


def answer_kernel(index_ref, asked_ref, table_ref, ahead_ref, out_ref, held_ref):
    width = table_ref.shape[1]

    def fetch(r, carry):
        held_ref[r, ROOM - 8 :, :] = jnp.zeros((8, width), jnp.float32)
        for s in range(CAP):
            held_ref[r, s : s + 1, :] = table_ref[pl.ds(index_ref[2 * r, s], 1), :]
        return carry

    lax.fori_loop(0, N_ROW, fetch, 0)
    line = lax.broadcasted_iota(jnp.int32, (DST, ROOM), 0) + 1
    gap = jnp.zeros((16, 128 - 3 * width), jnp.float32)
    for r in range(N_ROW):
        dest = asked_ref[2 * r + 1 : 2 * r + 2, :ROOM]
        place = jnp.where(dest == line, 1.0, 0.0).astype(jnp.bfloat16)
        value = held_ref[r]
        lead = value.astype(jnp.bfloat16)
        rest = (value - lead.astype(jnp.float32)).astype(jnp.bfloat16)
        total = jnp.dot(place, jnp.concatenate([lead, rest], axis=1), preferred_element_type=jnp.float32)
        total = total[:, :width] + total[:, width:]
        out_ref[r] = jnp.concatenate([total[:16], total[16:32], total[32:], gap], axis=1)


def answers(asked, table, ahead):
    width = table.shape[1]
    return pl.pallas_call(
        answer_kernel,
        in_specs=[SMEM, VMEM, VMEM, pl.BlockSpec(memory_space=pl.ANY)],
        out_specs=VMEM,
        out_shape=jax.ShapeDtypeStruct((N_ROW, 16, 128), jnp.float32),
        scratch_shapes=[pltpu.VMEM((N_ROW, ROOM, width), jnp.float32)],
        compiler_params=SMALL,
        name="answers",
    )(asked, asked, table, ahead)


def body(features, dest_feat, owner, local_row, w_self, w_neigh, grad_out):
    width = features.shape[1]
    hid = w_self.shape[1]
    asked = requests(owner.reshape(1, -1), local_row.reshape(1, -1))
    asked = exchange(asked.reshape(N_ROW, 2, SLOTS), ROW).reshape(2 * N_ROW, SLOTS)
    pre_self = jnp.dot(dest_feat, w_self, precision=HIGH)
    part = exchange(answers(asked, features, pre_self), ROW)
    part = jnp.sum(part, axis=0) / FAN
    agg = jnp.concatenate([part[:, k * width : (k + 1) * width] for k in range(DST // 16)], axis=0)
    pre = pre_self + jnp.dot(agg, w_neigh, precision=HIGH)
    pair = lax.all_gather(pre.reshape(2, DST // 2, hid), "core", axis=0, tiled=False)
    half = jnp.sum(lax.dynamic_index_in_dim(pair, lax.axis_index("core"), axis=1, keepdims=False), axis=0)
    half = half.reshape(3, 8, 4, 256).transpose(0, 2, 1, 3).reshape(N_Z, 8, 256)
    tile = jnp.sum(exchange(half, "z"), axis=0)
    half = exchange(jnp.broadcast_to(tile[None], (N_Z, 8, 256)), "z")
    half = half.reshape(3, 4, 8, 256).transpose(0, 2, 1, 3).reshape(DST // 2, hid)
    pre = lax.all_gather(half, "core", axis=0, tiled=True)
    hidden, slope = activate(pre)
    dpre = grad_out * slope
    both = jnp.concatenate([dest_feat.T, agg.T], axis=0)
    part = jnp.dot(both, dpre, precision=HIGH)
    part = part.reshape(4, 16, 8, 128).transpose(0, 2, 1, 3).reshape(N_ROW, 16, 128)
    total = jnp.sum(exchange(part, ROW), axis=0)
    grads = exchange(jnp.broadcast_to(total[None], (N_ROW, 16, 128)), ROW)
    grads = grads.reshape(4, 8, 16, 128).transpose(0, 2, 1, 3).reshape(64, hid)
    return (hidden, grads[:32], grads[32:])


def solution(mesh):
    grid = Mesh(mesh.devices.reshape(8, 4, 12, 2), ("y", "x", "z", "core"))
    return jax.shard_map(
        body,
        mesh=grid,
        in_specs=(P(ROW, COL), P(ROW, COL), P(ROW, None), P(ROW), P(COL, None), P(COL, None), P(ROW, None)),
        out_specs=(P(ROW, None), P(COL, None), P(COL, None)),
        check_vma=False,
    )
```

```python
import jax
import jax.numpy as jnp
from jax import lax
from jax.experimental import pallas as pl
from jax.experimental.pallas import tpu as pltpu
from jax.sharding import Mesh, PartitionSpec as P

FAN = 25
DST = 48
CAP = 75
ROOM = 80
SLOTS = 128
ROW = ("y", "x")
COL = ("z", "core")
N_ROW = 32
N_Z = 12
BEND = 0.7978845608
CUBE = 0.044715
HIGH = lax.Precision.HIGH
LANES = (((1,), (1,)), ((), ()))
VMEM = pl.BlockSpec(memory_space=pltpu.VMEM)
ANY = pl.BlockSpec(memory_space=pl.ANY)
SMEM = pl.BlockSpec(memory_space=pltpu.SMEM)
SMALL = pltpu.CompilerParams(vmem_limit_bytes=16 << 20)


def exchange(value, axis):
    return lax.all_to_all(value, axis, split_axis=0, concat_axis=0, tiled=True)


def request_kernel(owner_ref, row_ref, out_ref):
    samples = owner_ref.shape[1]
    blocks = -(-samples // 128)
    line = lax.broadcasted_iota(jnp.int32, (2 * N_ROW, 128), 0)
    lane = lax.broadcasted_iota(jnp.int32, (1, 128), 1)
    even = (line & 1) == 0
    before = lax.broadcasted_iota(jnp.int32, (128, 128), 0) >= lax.broadcasted_iota(jnp.int32, (128, 128), 1)
    before = jnp.where(before, 1.0, 0.0).astype(jnp.bfloat16)
    slot = lax.broadcasted_iota(jnp.int32, (SLOTS, 128), 0).astype(jnp.float32)

    def part(ref, block, fill):
        width = min(128, samples - block * 128)
        values = ref[:, block * 128 : block * 128 + width]
        if width < 128:
            values = jnp.concatenate([values, jnp.full((1, 128 - width), fill, jnp.int32)], axis=1)
        return values

    marks, counts = [], []
    for block in range(blocks):
        mark = part(owner_ref, block, -1) == (line >> 1)
        marks.append(mark)
        counts.append(
            lax.dot_general(
                jnp.where(mark, 1.0, 0.0).astype(jnp.bfloat16), before, LANES, preferred_element_type=jnp.float32
            )
        )
    seen = jnp.full((2 * N_ROW, 1), -1.0, jnp.float32)
    lefts, rights = [], []
    for block in range(blocks):
        rows = part(row_ref, block, 0)
        mark, count = marks[block], counts[block]
        rank = jnp.sum(jnp.where(mark & even, count + seen, 0.0), axis=0, keepdims=True)
        seen = seen + count[:, 127:128]
        rights.append(jnp.where(rank == slot, 1.0, 0.0).astype(jnp.bfloat16))
        dest = (lane + block * 128) // FAN + 1
        high = jnp.where(mark, jnp.where(even, rows >> 6, dest), 0).astype(jnp.float32)
        low = jnp.where(mark & even, rows & 63, 0).astype(jnp.float32)
        lefts.append(jnp.concatenate([high, low], axis=0).astype(jnp.bfloat16))
    total = lax.dot_general(
        jnp.concatenate(lefts, axis=1), jnp.concatenate(rights, axis=1), LANES, preferred_element_type=jnp.float32
    )
    first, second = total[: 2 * N_ROW], total[2 * N_ROW :]
    out_ref[...] = (jnp.where(even, first * 64.0, first) + second).astype(jnp.int32)


def requests(owner, local_row):
    return pl.pallas_call(
        request_kernel,
        in_specs=[VMEM, VMEM],
        out_specs=VMEM,
        out_shape=jax.ShapeDtypeStruct((2 * N_ROW, SLOTS), jnp.int32),
        compiler_params=SMALL,
        name="requests",
    )(owner, local_row)


def answer_kernel(index_ref, asked_ref, table_ref, ahead_ref, core_ref, out_ref, held_ref):
    width = table_ref.shape[1]

    def fetch(r, carry):
        held_ref[r, ROOM - 8 :, :] = jnp.zeros((8, width), jnp.float32)
        for s in range(CAP):
            held_ref[r, s : s + 1, :] = table_ref[pl.ds(index_ref[2 * r, s], 1), :]
        return carry

    lax.fori_loop(0, N_ROW, fetch, 0)
    line = lax.broadcasted_iota(jnp.int32, (DST, ROOM), 0) + 1
    gap = jnp.zeros((16, 128 - 3 * width), jnp.float32)
    for r in range(N_ROW):
        dest = asked_ref[2 * r + 1 : 2 * r + 2, :ROOM]
        place = jnp.where(dest == line, 1.0, 0.0).astype(jnp.bfloat16)
        value = held_ref[r]
        lead = value.astype(jnp.bfloat16)
        rest = (value - lead.astype(jnp.float32)).astype(jnp.bfloat16)
        total = jnp.dot(place, jnp.concatenate([lead, rest], axis=1), preferred_element_type=jnp.float32)
        total = total[:, :width] + total[:, width:]
        out_ref[r] = jnp.concatenate([total[:16], total[16:32], total[32:], gap], axis=1)


def answers(asked, table, ahead, core):
    width = table.shape[1]
    return pl.pallas_call(
        answer_kernel,
        in_specs=[SMEM, VMEM, VMEM, ANY, ANY],
        out_specs=VMEM,
        out_shape=jax.ShapeDtypeStruct((N_ROW, 16, 128), jnp.float32),
        scratch_shapes=[pltpu.VMEM((N_ROW, ROOM, width), jnp.float32)],
        compiler_params=SMALL,
        name="answers",
    )(asked, asked, table, ahead, core)


def split(value):
    lead = value.astype(jnp.bfloat16)
    return lead, (value - lead.astype(jnp.float32)).astype(jnp.bfloat16)


def gradient_kernel(pre_ref, grad_ref, own_ref, part_ref, hidden_ref, out_ref):
    width, hid = own_ref.shape[0], pre_ref.shape[1]
    turned = part_ref[...].T
    agg = jnp.concatenate([turned[k * width : (k + 1) * width] for k in range(DST // 16)], axis=1)
    lead, rest = split(jnp.concatenate([own_ref[...], agg], axis=0))
    both = jnp.concatenate([lead, rest], axis=0)
    step = 256
    for at in range(hid // step):
        value = pre_ref[:, at * step : (at + 1) * step]
        square = value * value
        bent = jnp.tanh(BEND * (value + CUBE * (value * square)))
        hidden_ref[:, at * step : (at + 1) * step] = (0.5 * value) * (1.0 + bent)
        slope = 0.5 * (1.0 + bent) + (0.5 * value) * (1.0 - bent * bent) * (BEND * (1.0 + (3.0 * CUBE) * square))
        high, low = split(grad_ref[:, at * step : (at + 1) * step] * slope)
        total = jnp.dot(both, high, preferred_element_type=jnp.float32)
        total = total[: 2 * width] + total[2 * width :] + jnp.dot(lead, low, preferred_element_type=jnp.float32)
        for line in range(4):
            for lane in range(step // 128):
                out_ref[line * (hid // 128) + at * (step // 128) + lane] = total[
                    line * 16 : line * 16 + 16, lane * 128 : lane * 128 + 128
                ]


def gradients(pre, grad_out, own, part):
    return pl.pallas_call(
        gradient_kernel,
        in_specs=[VMEM] * 4,
        out_specs=[VMEM] * 2,
        out_shape=[
            jax.ShapeDtypeStruct(pre.shape, jnp.float32),
            jax.ShapeDtypeStruct((N_ROW, 16, 128), jnp.float32),
        ],
        compiler_params=SMALL,
        name="gradients",
    )(pre, grad_out, own, part)


def body(features, dest_feat, owner, local_row, w_self, w_neigh, grad_out):
    width = features.shape[1]
    hid = w_self.shape[1]
    asked = requests(owner.reshape(1, -1), local_row.reshape(1, -1))
    asked = exchange(asked.reshape(N_ROW, 2, SLOTS), ROW).reshape(2 * N_ROW, SLOTS)
    pre_self = jnp.dot(dest_feat, w_self, precision=HIGH)
    core = lax.axis_index("core")
    part = exchange(answers(asked, features, pre_self, core.reshape(1)), ROW)
    part = jnp.sum(part, axis=0) / FAN
    agg = jnp.concatenate([part[:, k * width : (k + 1) * width] for k in range(DST // 16)], axis=0)
    pre = pre_self + jnp.dot(agg, w_neigh, precision=HIGH)
    pair = lax.all_gather(pre.reshape(2, DST // 2, hid), "core", axis=0, tiled=False)
    half = jnp.sum(lax.dynamic_index_in_dim(pair, core, axis=1, keepdims=False, allow_negative_indices=False), axis=0)
    half = half.reshape(3, 8, 4, 256).transpose(0, 2, 1, 3).reshape(N_Z, 8, 256)
    tile = jnp.sum(exchange(half, "z"), axis=0)
    half = exchange(jnp.broadcast_to(tile[None], (N_Z, 8, 256)), "z")
    half = half.reshape(3, 4, 8, 256).transpose(0, 2, 1, 3).reshape(DST // 2, hid)
    pre = lax.all_gather(half, "core", axis=0, tiled=True)
    hidden, part = gradients(pre, grad_out, dest_feat.T, part)
    total = jnp.sum(exchange(part, ROW), axis=0)
    grads = exchange(jnp.broadcast_to(total[None], (N_ROW, 16, 128)), ROW)
    grads = grads.reshape(4, 8, 16, 128).transpose(0, 2, 1, 3).reshape(64, hid)
    return (hidden, grads[:32], grads[32:])


def solution(mesh):
    grid = Mesh(mesh.devices.reshape(8, 4, 12, 2), ("y", "x", "z", "core"))
    return jax.shard_map(
        body,
        mesh=grid,
        in_specs=(P(ROW, COL), P(ROW, COL), P(ROW, None), P(ROW), P(COL, None), P(COL, None), P(ROW, None)),
        out_specs=(P(ROW, None), P(COL, None), P(COL, None)),
        check_vma=False,
    )
```

```python
import jax
import jax.numpy as jnp
from jax import lax
from jax.experimental import pallas as pl
from jax.experimental.pallas import tpu as pltpu
from jax.sharding import Mesh, PartitionSpec as P

FAN = 25
DST = 48
CAP = 75
ROOM = 80
SLOTS = 128
ROW = ("y", "x")
COL = ("z", "core")
N_ROW = 32
N_Z = 12
BEND = 0.7978845608
CUBE = 0.044715
LANES = (((1,), (1,)), ((), ()))
VMEM = pl.BlockSpec(memory_space=pltpu.VMEM)
ANY = pl.BlockSpec(memory_space=pl.ANY)
HBM = pl.BlockSpec(memory_space=pltpu.HBM)
SMEM = pl.BlockSpec(memory_space=pltpu.SMEM)
SMALL = pltpu.CompilerParams(vmem_limit_bytes=16 << 20)


def exchange(value, axis):
    return lax.all_to_all(value, axis, split_axis=0, concat_axis=0, tiled=True)


def request_kernel(owner_from, row_from, out_ref, owner_ref, row_ref, sems):
    loads = [
        pltpu.make_async_copy(owner_from, owner_ref, sems.at[0]),
        pltpu.make_async_copy(row_from, row_ref, sems.at[1]),
    ]
    for load in loads:
        load.start()
    samples = owner_ref.shape[1]
    blocks = -(-samples // 128)
    line = lax.broadcasted_iota(jnp.int32, (2 * N_ROW, 128), 0)
    lane = lax.broadcasted_iota(jnp.int32, (1, 128), 1)
    even = (line & 1) == 0
    before = lax.broadcasted_iota(jnp.int32, (128, 128), 0) >= lax.broadcasted_iota(jnp.int32, (128, 128), 1)
    before = jnp.where(before, 1.0, 0.0).astype(jnp.bfloat16)
    slot = lax.broadcasted_iota(jnp.int32, (SLOTS, 128), 0).astype(jnp.float32)

    def padded(values, fill):
        width = values.shape[1]
        if width < 128:
            values = jnp.concatenate([values, jnp.full((1, 128 - width), fill, jnp.int32)], axis=1)
        return values

    for load in loads:
        load.wait()
    marks, counts = [], []
    for block in range(blocks):
        end = min(samples, block * 128 + 128)
        mark = padded(owner_ref[:, block * 128 : end], -1) == (line >> 1)
        marks.append(mark)
        counts.append(
            lax.dot_general(
                jnp.where(mark, 1.0, 0.0).astype(jnp.bfloat16), before, LANES, preferred_element_type=jnp.float32
            )
        )
    seen = jnp.full((2 * N_ROW, 1), -1.0, jnp.float32)
    lefts, rights = [], []
    for block in range(blocks):
        end = min(samples, block * 128 + 128)
        rows = padded(row_ref[block * 128 : end].reshape(1, -1), 0)
        mark, count = marks[block], counts[block]
        rank = jnp.sum(jnp.where(mark & even, count + seen, 0.0), axis=0, keepdims=True)
        seen = seen + count[:, 127:128]
        rights.append(jnp.where(rank == slot, 1.0, 0.0).astype(jnp.bfloat16))
        dest = (lane + block * 128) // FAN + 1
        high = jnp.where(mark, jnp.where(even, rows >> 6, dest), 0).astype(jnp.float32)
        low = jnp.where(mark & even, rows & 63, 0).astype(jnp.float32)
        lefts.append(jnp.concatenate([high, low], axis=0).astype(jnp.bfloat16))
    total = lax.dot_general(
        jnp.concatenate(lefts, axis=1), jnp.concatenate(rights, axis=1), LANES, preferred_element_type=jnp.float32
    )
    first, second = total[: 2 * N_ROW], total[2 * N_ROW :]
    out_ref[...] = (jnp.where(even, first * 64.0, first) + second).astype(jnp.int32)


def requests(owner, local_row):
    return pl.pallas_call(
        request_kernel,
        in_specs=[HBM, HBM],
        out_specs=VMEM,
        out_shape=jax.ShapeDtypeStruct((2 * N_ROW, SLOTS), jnp.int32),
        scratch_shapes=[
            pltpu.VMEM(owner.shape, jnp.int32),
            pltpu.VMEM(local_row.shape, jnp.int32),
            pltpu.SemaphoreType.DMA((2,)),
        ],
        name="requests",
    )(owner, local_row)


def answer_kernel(index_ref, asked_ref, table_ref, core_ref, out_ref, held_ref):
    width = table_ref.shape[1]

    def fetch(r, carry):
        held_ref[r, ROOM - 8 :, :] = jnp.zeros((8, width), jnp.float32)
        for s in range(CAP):
            held_ref[r, s : s + 1, :] = table_ref[pl.ds(index_ref[2 * r, s], 1), :]
        return carry

    lax.fori_loop(0, N_ROW, fetch, 0)
    line = lax.broadcasted_iota(jnp.int32, (DST, ROOM), 0) + 1
    gap = jnp.zeros((16, 128 - 3 * width), jnp.float32)
    for r in range(N_ROW):
        dest = asked_ref[2 * r + 1 : 2 * r + 2, :ROOM]
        place = jnp.where(dest == line, 1.0, 0.0).astype(jnp.bfloat16)
        value = held_ref[r]
        lead = value.astype(jnp.bfloat16)
        rest = (value - lead.astype(jnp.float32)).astype(jnp.bfloat16)
        total = jnp.dot(place, jnp.concatenate([lead, rest], axis=1), preferred_element_type=jnp.float32)
        total = total[:, :width] + total[:, width:]
        out_ref[r] = jnp.concatenate([total[:16], total[16:32], total[32:], gap], axis=1)


def answers(asked, table, core):
    width = table.shape[1]
    return pl.pallas_call(
        answer_kernel,
        in_specs=[SMEM, VMEM, VMEM, ANY],
        out_specs=VMEM,
        out_shape=jax.ShapeDtypeStruct((N_ROW, 16, 128), jnp.float32),
        scratch_shapes=[pltpu.VMEM((N_ROW, ROOM, width), jnp.float32)],
        compiler_params=SMALL,
        name="answers",
    )(asked, asked, table, core)


def split(value):
    lead = value.astype(jnp.bfloat16)
    return lead, (value - lead.astype(jnp.float32)).astype(jnp.bfloat16)


def product(left, right):
    lead, rest = split(left)
    high, low = split(right)
    total = jnp.dot(jnp.concatenate([lead, rest], axis=0), high, preferred_element_type=jnp.float32)
    lines = left.shape[0]
    return total[:lines] + total[lines:] + jnp.dot(lead, low, preferred_element_type=jnp.float32)


def project_kernel(part_ref, own_ref, self_ref, neigh_ref, agg_ref, out_ref):
    width, hid = self_ref.shape
    total = part_ref[0]
    for r in range(1, N_ROW):
        total = total + part_ref[r]
    total = total / FAN
    agg_ref[...] = total
    agg = jnp.concatenate([total[:, k * width : (k + 1) * width] for k in range(DST // 16)], axis=0)
    both = jnp.concatenate([own_ref[...].T, agg], axis=1)
    step = 256
    for at in range(0, hid, step):
        weight = jnp.concatenate([self_ref[:, at : at + step], neigh_ref[:, at : at + step]], axis=0)
        out_ref[:, at : at + step] = product(both, weight)


def project(part, own, w_self, w_neigh):
    return pl.pallas_call(
        project_kernel,
        in_specs=[VMEM] * 4,
        out_specs=[VMEM] * 2,
        out_shape=[
            jax.ShapeDtypeStruct(part.shape[1:], jnp.float32),
            jax.ShapeDtypeStruct((DST, w_self.shape[1]), jnp.float32),
        ],
        compiler_params=SMALL,
        name="project",
    )(part, own, w_self, w_neigh)


def gradient_kernel(pre_ref, grad_ref, own_ref, part_ref, hidden_ref, out_ref):
    width, hid = own_ref.shape[0], pre_ref.shape[1]
    turned = part_ref[...].T
    agg = jnp.concatenate([turned[k * width : (k + 1) * width] for k in range(DST // 16)], axis=1)
    lead, rest = split(jnp.concatenate([own_ref[...], agg], axis=0))
    both = jnp.concatenate([lead, rest], axis=0)
    step = 256
    for at in range(hid // step):
        value = pre_ref[:, at * step : (at + 1) * step]
        square = value * value
        bent = jnp.tanh(BEND * (value + CUBE * (value * square)))
        hidden_ref[:, at * step : (at + 1) * step] = (0.5 * value) * (1.0 + bent)
        slope = 0.5 * (1.0 + bent) + (0.5 * value) * (1.0 - bent * bent) * (BEND * (1.0 + (3.0 * CUBE) * square))
        high, low = split(grad_ref[:, at * step : (at + 1) * step] * slope)
        total = jnp.dot(both, high, preferred_element_type=jnp.float32)
        total = total[: 2 * width] + total[2 * width :] + jnp.dot(lead, low, preferred_element_type=jnp.float32)
        for line in range(4):
            for lane in range(step // 128):
                out_ref[line * (hid // 128) + at * (step // 128) + lane] = total[
                    line * 16 : line * 16 + 16, lane * 128 : lane * 128 + 128
                ]


def gradients(pre, grad_out, own, part):
    return pl.pallas_call(
        gradient_kernel,
        in_specs=[VMEM] * 4,
        out_specs=[VMEM] * 2,
        out_shape=[
            jax.ShapeDtypeStruct(pre.shape, jnp.float32),
            jax.ShapeDtypeStruct((N_ROW, 16, 128), jnp.float32),
        ],
        compiler_params=SMALL,
        name="gradients",
    )(pre, grad_out, own, part)


def body(features, dest_feat, owner, local_row, w_self, w_neigh, grad_out):
    hid = w_self.shape[1]
    asked = requests(owner.reshape(1, -1), local_row)
    asked = exchange(asked.reshape(N_ROW, 2, SLOTS), ROW).reshape(2 * N_ROW, SLOTS)
    core = lax.axis_index("core")
    own = dest_feat.T
    part = exchange(answers(asked, features, core.reshape(1)), ROW)
    agg, pre = project(part, own, w_self, w_neigh)
    pair = lax.all_gather(pre.reshape(2, DST // 2, hid), "core", axis=0, tiled=False)
    half = jnp.sum(lax.dynamic_index_in_dim(pair, core, axis=1, keepdims=False, allow_negative_indices=False), axis=0)
    half = half.reshape(3, 8, 4, 256).transpose(0, 2, 1, 3).reshape(N_Z, 8, 256)
    tile = jnp.sum(exchange(half, "z"), axis=0)
    half = exchange(jnp.broadcast_to(tile[None], (N_Z, 8, 256)), "z")
    half = half.reshape(3, 4, 8, 256).transpose(0, 2, 1, 3).reshape(DST // 2, hid)
    pre = lax.all_gather(half, "core", axis=0, tiled=True)
    hidden, part = gradients(pre, grad_out, own, agg)
    total = jnp.sum(exchange(part, ROW), axis=0)
    grads = exchange(jnp.broadcast_to(total[None], (N_ROW, 16, 128)), ROW)
    grads = grads.reshape(4, 8, 16, 128).transpose(0, 2, 1, 3).reshape(64, hid)
    return (hidden, grads[:32], grads[32:])


def solution(mesh):
    grid = Mesh(mesh.devices.reshape(8, 4, 12, 2), ("y", "x", "z", "core"))
    return jax.shard_map(
        body,
        mesh=grid,
        in_specs=(P(ROW, COL), P(ROW, COL), P(ROW, None), P(ROW), P(COL, None), P(COL, None), P(ROW, None)),
        out_specs=(P(ROW, None), P(COL, None), P(COL, None)),
        check_vma=False,
    )
```

```python
import jax
import jax.numpy as jnp
from jax import lax
from jax.experimental import pallas as pl
from jax.experimental.pallas import tpu as pltpu
from jax.sharding import Mesh, PartitionSpec as P

FAN = 25
DST = 48
CAP = 75
ROOM = 80
SLOTS = 128
ROW = ("y", "x")
COL = ("z", "core")
N_ROW = 32
N_Z = 12
BEND = 0.7978845608
CUBE = 0.044715
LANES = (((1,), (1,)), ((), ()))
VMEM = pl.BlockSpec(memory_space=pltpu.VMEM)
ANY = pl.BlockSpec(memory_space=pl.ANY)
HBM = pl.BlockSpec(memory_space=pltpu.HBM)
SMALL = pltpu.CompilerParams(vmem_limit_bytes=16 << 20)


def exchange(value, axis):
    return lax.all_to_all(value, axis, split_axis=0, concat_axis=0, tiled=True)


def request_kernel(owner_from, row_from, out_ref, owner_ref, row_ref, sems):
    loads = [
        pltpu.make_async_copy(owner_from, owner_ref, sems.at[0]),
        pltpu.make_async_copy(row_from, row_ref, sems.at[1]),
    ]
    for load in loads:
        load.start()
    samples = owner_ref.shape[1]
    blocks = -(-samples // 128)
    line = lax.broadcasted_iota(jnp.int32, (2 * N_ROW, 128), 0)
    lane = lax.broadcasted_iota(jnp.int32, (1, 128), 1)
    even = (line & 1) == 0
    before = lax.broadcasted_iota(jnp.int32, (128, 128), 0) >= lax.broadcasted_iota(jnp.int32, (128, 128), 1)
    before = jnp.where(before, 1.0, 0.0).astype(jnp.bfloat16)
    slot = lax.broadcasted_iota(jnp.int32, (SLOTS, 128), 0).astype(jnp.float32)

    def padded(values, fill):
        width = values.shape[1]
        if width < 128:
            values = jnp.concatenate([values, jnp.full((1, 128 - width), fill, jnp.int32)], axis=1)
        return values

    for load in loads:
        load.wait()
    marks, counts = [], []
    for block in range(blocks):
        end = min(samples, block * 128 + 128)
        mark = padded(owner_ref[:, block * 128 : end], -1) == (line >> 1)
        marks.append(mark)
        counts.append(
            lax.dot_general(
                jnp.where(mark, 1.0, 0.0).astype(jnp.bfloat16), before, LANES, preferred_element_type=jnp.float32
            )
        )
    seen = jnp.full((2 * N_ROW, 1), -1.0, jnp.float32)
    lefts, rights = [], []
    for block in range(blocks):
        end = min(samples, block * 128 + 128)
        rows = padded(row_ref[block * 128 : end].reshape(1, -1), 0)
        mark, count = marks[block], counts[block]
        rank = jnp.sum(jnp.where(mark & even, count + seen, 0.0), axis=0, keepdims=True)
        seen = seen + count[:, 127:128]
        rights.append(jnp.where(rank == slot, 1.0, 0.0).astype(jnp.bfloat16))
        dest = (lane + block * 128) // FAN + 1
        high = jnp.where(mark, jnp.where(even, rows >> 6, dest), 0).astype(jnp.float32)
        low = jnp.where(mark & even, rows & 63, 0).astype(jnp.float32)
        lefts.append(jnp.concatenate([high, low], axis=0).astype(jnp.bfloat16))
    total = lax.dot_general(
        jnp.concatenate(lefts, axis=1), jnp.concatenate(rights, axis=1), LANES, preferred_element_type=jnp.float32
    )
    first, second = total[: 2 * N_ROW], total[2 * N_ROW :]
    out_ref[...] = (jnp.where(even, first * 64.0, first) + second).astype(jnp.int32)


def requests(owner, local_row):
    return pl.pallas_call(
        request_kernel,
        in_specs=[HBM, HBM],
        out_specs=VMEM,
        out_shape=jax.ShapeDtypeStruct((2 * N_ROW, SLOTS), jnp.int32),
        scratch_shapes=[
            pltpu.VMEM(owner.shape, jnp.int32),
            pltpu.VMEM(local_row.shape, jnp.int32),
            pltpu.SemaphoreType.DMA((2,)),
        ],
        name="requests",
    )(owner, local_row)


def answer_kernel(index_from, asked_ref, table_ref, core_ref, out_ref, held_ref, place_ref, index_ref, sem):
    width = table_ref.shape[1]
    load = pltpu.make_async_copy(index_from, index_ref, sem)
    load.start()
    line = lax.broadcasted_iota(jnp.int32, (DST, ROOM), 0) + 1
    for r in range(N_ROW):
        dest = asked_ref[2 * r + 1 : 2 * r + 2, :ROOM]
        place_ref[r] = jnp.where(dest == line, 1.0, 0.0).astype(jnp.bfloat16)
        held_ref[r, ROOM - 8 :, :] = jnp.zeros((8, width), jnp.float32)
    load.wait()

    def fetch(r, carry):
        for s in range(CAP):
            held_ref[r, s : s + 1, :] = table_ref[pl.ds(index_ref[r * CAP + s], 1), :]
        return carry

    lax.fori_loop(0, N_ROW, fetch, 0)
    gap = jnp.zeros((16, 128 - 3 * width), jnp.float32)
    for r in range(N_ROW):
        lead, rest = split(held_ref[r])
        total = jnp.dot(place_ref[r], jnp.concatenate([lead, rest], axis=1), preferred_element_type=jnp.float32)
        total = total[:, :width] + total[:, width:]
        out_ref[r] = jnp.concatenate([total[:16], total[16:32], total[32:], gap], axis=1)


def answers(asked, table, core):
    width = table.shape[1]
    index = asked.reshape(N_ROW, 2, SLOTS)[:, 0, :CAP].reshape(-1)
    return pl.pallas_call(
        answer_kernel,
        in_specs=[VMEM, VMEM, VMEM, ANY],
        out_specs=VMEM,
        out_shape=jax.ShapeDtypeStruct((N_ROW, 16, 128), jnp.float32),
        scratch_shapes=[
            pltpu.VMEM((N_ROW, ROOM, width), jnp.float32),
            pltpu.VMEM((N_ROW, DST, ROOM), jnp.bfloat16),
            pltpu.SMEM(index.shape, jnp.int32),
            pltpu.SemaphoreType.DMA,
        ],
        compiler_params=SMALL,
        name="answers",
    )(index, asked, table, core)


def split(value):
    lead = value.astype(jnp.bfloat16)
    return lead, (value - lead.astype(jnp.float32)).astype(jnp.bfloat16)


def product(left, right):
    lead, rest = split(left)
    high, low = split(right)
    total = jnp.dot(jnp.concatenate([lead, rest], axis=0), high, preferred_element_type=jnp.float32)
    lines = left.shape[0]
    return total[:lines] + total[lines:] + jnp.dot(lead, low, preferred_element_type=jnp.float32)


def project_kernel(part_ref, own_ref, self_ref, neigh_ref, agg_ref, out_ref):
    width, hid = self_ref.shape
    total = part_ref[0]
    for r in range(1, N_ROW):
        total = total + part_ref[r]
    total = total / FAN
    agg_ref[...] = total
    agg = jnp.concatenate([total[:, k * width : (k + 1) * width] for k in range(DST // 16)], axis=0)
    both = jnp.concatenate([own_ref[...].T, agg], axis=1)
    step = 256
    for at in range(0, hid, step):
        weight = jnp.concatenate([self_ref[:, at : at + step], neigh_ref[:, at : at + step]], axis=0)
        out_ref[:, at : at + step] = product(both, weight)


def project(part, own, w_self, w_neigh):
    return pl.pallas_call(
        project_kernel,
        in_specs=[VMEM] * 4,
        out_specs=[VMEM] * 2,
        out_shape=[
            jax.ShapeDtypeStruct(part.shape[1:], jnp.float32),
            jax.ShapeDtypeStruct((DST, w_self.shape[1]), jnp.float32),
        ],
        compiler_params=SMALL,
        name="project",
    )(part, own, w_self, w_neigh)


def gradient_kernel(pre_ref, grad_ref, own_ref, part_ref, hidden_ref, out_ref):
    width, hid = own_ref.shape[0], pre_ref.shape[1]
    turned = part_ref[...].T
    agg = jnp.concatenate([turned[k * width : (k + 1) * width] for k in range(DST // 16)], axis=1)
    lead, rest = split(jnp.concatenate([own_ref[...], agg], axis=0))
    both = jnp.concatenate([lead, rest], axis=0)
    step = 256
    for at in range(hid // step):
        value = pre_ref[:, at * step : (at + 1) * step]
        square = value * value
        bent = jnp.tanh(BEND * (value + CUBE * (value * square)))
        hidden_ref[:, at * step : (at + 1) * step] = (0.5 * value) * (1.0 + bent)
        slope = 0.5 * (1.0 + bent) + (0.5 * value) * (1.0 - bent * bent) * (BEND * (1.0 + (3.0 * CUBE) * square))
        high, low = split(grad_ref[:, at * step : (at + 1) * step] * slope)
        total = jnp.dot(both, high, preferred_element_type=jnp.float32)
        total = total[: 2 * width] + total[2 * width :] + jnp.dot(lead, low, preferred_element_type=jnp.float32)
        for line in range(4):
            for lane in range(step // 128):
                out_ref[line * (hid // 128) + at * (step // 128) + lane] = total[
                    line * 16 : line * 16 + 16, lane * 128 : lane * 128 + 128
                ]


def gradients(pre, grad_out, own, part):
    return pl.pallas_call(
        gradient_kernel,
        in_specs=[VMEM] * 4,
        out_specs=[VMEM] * 2,
        out_shape=[
            jax.ShapeDtypeStruct(pre.shape, jnp.float32),
            jax.ShapeDtypeStruct((N_ROW, 16, 128), jnp.float32),
        ],
        compiler_params=SMALL,
        name="gradients",
    )(pre, grad_out, own, part)


def spread_kernel(block_ref, self_ref, neigh_ref):
    lanes = self_ref.shape[1] // 128
    for at, out_ref in ((0, self_ref), (1, neigh_ref)):
        for line in range(2):
            for lane in range(lanes):
                out_ref[line * 16 : line * 16 + 16, lane * 128 : lane * 128 + 128] = block_ref[
                    (2 * at + line) * lanes + lane
                ]


def spread(blocks, hid):
    return pl.pallas_call(
        spread_kernel,
        in_specs=[VMEM],
        out_specs=[VMEM] * 2,
        out_shape=[jax.ShapeDtypeStruct((32, hid), jnp.float32)] * 2,
        compiler_params=SMALL,
        name="spread",
    )(blocks)


def body(features, dest_feat, owner, local_row, w_self, w_neigh, grad_out):
    hid = w_self.shape[1]
    asked = requests(owner.reshape(1, -1), local_row)
    asked = exchange(asked.reshape(N_ROW, 2, SLOTS), ROW).reshape(2 * N_ROW, SLOTS)
    core = lax.axis_index("core")
    own = dest_feat.T
    part = exchange(answers(asked, features, core.reshape(1)), ROW)
    agg, pre = project(part, own, w_self, w_neigh)
    pair = lax.all_gather(pre.reshape(2, DST // 2, hid), "core", axis=0, tiled=False)
    half = jnp.sum(lax.dynamic_index_in_dim(pair, core, axis=1, keepdims=False, allow_negative_indices=False), axis=0)
    half = half.reshape(3, 8, 4, 256).transpose(0, 2, 1, 3).reshape(N_Z, 8, 256)
    tile = jnp.sum(exchange(half, "z"), axis=0)
    half = exchange(jnp.broadcast_to(tile[None], (N_Z, 8, 256)), "z")
    half = half.reshape(3, 4, 8, 256).transpose(0, 2, 1, 3).reshape(DST // 2, hid)
    pre = lax.all_gather(half, "core", axis=0, tiled=True)
    hidden, part = gradients(pre, grad_out, own, agg)
    total = jnp.sum(exchange(part, ROW), axis=0)
    grads = exchange(jnp.broadcast_to(total[None], (N_ROW, 16, 128)), ROW)
    return (hidden, *spread(grads, hid))


def solution(mesh):
    grid = Mesh(mesh.devices.reshape(8, 4, 12, 2), ("y", "x", "z", "core"))
    return jax.shard_map(
        body,
        mesh=grid,
        in_specs=(P(ROW, COL), P(ROW, COL), P(ROW, None), P(ROW), P(COL, None), P(COL, None), P(ROW, None)),
        out_specs=(P(ROW, None), P(COL, None), P(COL, None)),
        check_vma=False,
    )
```

```python
import jax
import jax.numpy as jnp
from jax import lax
from jax.experimental import pallas as pl
from jax.experimental.pallas import tpu as pltpu
from jax.sharding import Mesh, PartitionSpec as P

FAN = 25
DST = 48
CAP = 75
ROOM = 80
SLOTS = 128
ROW = ("y", "x")
ACROSS = ("x", "y")
COL = ("z", "core")
N_ROW = 32
N_Z = 12
BEND = 0.7978845608
CUBE = 0.044715
LANES = (((1,), (1,)), ((), ()))
VMEM = pl.BlockSpec(memory_space=pltpu.VMEM)
ANY = pl.BlockSpec(memory_space=pl.ANY)
HBM = pl.BlockSpec(memory_space=pltpu.HBM)
SMALL = pltpu.CompilerParams(vmem_limit_bytes=16 << 20)


def exchange(value, axis):
    return lax.all_to_all(value, axis, split_axis=0, concat_axis=0, tiled=True)


def request_kernel(owner_from, row_from, out_ref, owner_ref, row_ref, sems):
    loads = [
        pltpu.make_async_copy(owner_from, owner_ref, sems.at[0]),
        pltpu.make_async_copy(row_from, row_ref, sems.at[1]),
    ]
    for load in loads:
        load.start()
    samples = owner_ref.shape[1]
    blocks = -(-samples // 128)
    line = lax.broadcasted_iota(jnp.int32, (2 * N_ROW, 128), 0)
    lane = lax.broadcasted_iota(jnp.int32, (1, 128), 1)
    even = (line & 1) == 0
    before = lax.broadcasted_iota(jnp.int32, (128, 128), 0) >= lax.broadcasted_iota(jnp.int32, (128, 128), 1)
    before = jnp.where(before, 1.0, 0.0).astype(jnp.bfloat16)
    slot = lax.broadcasted_iota(jnp.int32, (SLOTS, 128), 0).astype(jnp.float32)

    def padded(values, fill):
        width = values.shape[1]
        if width < 128:
            values = jnp.concatenate([values, jnp.full((1, 128 - width), fill, jnp.int32)], axis=1)
        return values

    for load in loads:
        load.wait()
    marks, counts = [], []
    for block in range(blocks):
        end = min(samples, block * 128 + 128)
        owners = padded(owner_ref[:, block * 128 : end], -1)
        mark = ((owners & 3) * 8 + (owners >> 2)) == (line >> 1)
        marks.append(mark)
        counts.append(
            lax.dot_general(
                jnp.where(mark, 1.0, 0.0).astype(jnp.bfloat16), before, LANES, preferred_element_type=jnp.float32
            )
        )
    seen = jnp.full((2 * N_ROW, 1), -1.0, jnp.float32)
    lefts, rights = [], []
    for block in range(blocks):
        end = min(samples, block * 128 + 128)
        rows = padded(row_ref[block * 128 : end].reshape(1, -1), 0)
        mark, count = marks[block], counts[block]
        rank = jnp.sum(jnp.where(mark & even, count + seen, 0.0), axis=0, keepdims=True)
        seen = seen + count[:, 127:128]
        rights.append(jnp.where(rank == slot, 1.0, 0.0).astype(jnp.bfloat16))
        dest = (lane + block * 128) // FAN + 1
        high = jnp.where(mark, jnp.where(even, rows >> 6, dest), 0).astype(jnp.float32)
        low = jnp.where(mark & even, rows & 63, 0).astype(jnp.float32)
        lefts.append(jnp.concatenate([high, low], axis=0).astype(jnp.bfloat16))
    total = lax.dot_general(
        jnp.concatenate(lefts, axis=1), jnp.concatenate(rights, axis=1), LANES, preferred_element_type=jnp.float32
    )
    first, second = total[: 2 * N_ROW], total[2 * N_ROW :]
    out_ref[...] = (jnp.where(even, first * 64.0, first) + second).astype(jnp.int32)


def requests(owner, local_row):
    return pl.pallas_call(
        request_kernel,
        in_specs=[HBM, HBM],
        out_specs=VMEM,
        out_shape=jax.ShapeDtypeStruct((2 * N_ROW, SLOTS), jnp.int32),
        scratch_shapes=[
            pltpu.VMEM(owner.shape, jnp.int32),
            pltpu.VMEM(local_row.shape, jnp.int32),
            pltpu.SemaphoreType.DMA((2,)),
        ],
        name="requests",
    )(owner, local_row)


def answer_kernel(index_from, asked_ref, table_ref, core_ref, out_ref, held_ref, place_ref, index_ref, sem):
    width = table_ref.shape[1]
    load = pltpu.make_async_copy(index_from, index_ref, sem)
    load.start()
    line = lax.broadcasted_iota(jnp.int32, (DST, ROOM), 0) + 1
    for r in range(N_ROW):
        dest = asked_ref[2 * r + 1 : 2 * r + 2, :ROOM]
        place_ref[r] = jnp.where(dest == line, 1.0, 0.0).astype(jnp.bfloat16)
        held_ref[r, ROOM - 8 :, :] = jnp.zeros((8, width), jnp.float32)
    load.wait()

    def fetch(r, carry):
        for s in range(CAP):
            held_ref[r, s : s + 1, :] = table_ref[pl.ds(index_ref[r * CAP + s], 1), :]
        return carry

    lax.fori_loop(0, N_ROW, fetch, 0)
    gap = jnp.zeros((16, 128 - 3 * width), jnp.float32)
    for r in range(N_ROW):
        lead, rest = split(held_ref[r])
        total = jnp.dot(place_ref[r], jnp.concatenate([lead, rest], axis=1), preferred_element_type=jnp.float32)
        total = total[:, :width] + total[:, width:]
        out_ref[r] = jnp.concatenate([total[:16], total[16:32], total[32:], gap], axis=1)


def answers(asked, table, core):
    width = table.shape[1]
    index = asked.reshape(N_ROW, 2, SLOTS)[:, 0, :CAP].reshape(-1)
    return pl.pallas_call(
        answer_kernel,
        in_specs=[VMEM, VMEM, VMEM, ANY],
        out_specs=VMEM,
        out_shape=jax.ShapeDtypeStruct((N_ROW, 16, 128), jnp.float32),
        scratch_shapes=[
            pltpu.VMEM((N_ROW, ROOM, width), jnp.float32),
            pltpu.VMEM((N_ROW, DST, ROOM), jnp.bfloat16),
            pltpu.SMEM(index.shape, jnp.int32),
            pltpu.SemaphoreType.DMA,
        ],
        compiler_params=SMALL,
        name="answers",
    )(index, asked, table, core)


def split(value):
    lead = value.astype(jnp.bfloat16)
    return lead, (value - lead.astype(jnp.float32)).astype(jnp.bfloat16)


def product(left, right):
    lead, rest = split(left)
    high, low = split(right)
    total = jnp.dot(jnp.concatenate([lead, rest], axis=0), high, preferred_element_type=jnp.float32)
    lines = left.shape[0]
    return total[:lines] + total[lines:] + jnp.dot(lead, low, preferred_element_type=jnp.float32)


def project_kernel(part_ref, own_ref, self_ref, neigh_ref, agg_ref, out_ref):
    width, hid = self_ref.shape
    total = part_ref[0]
    for r in range(1, N_ROW):
        total = total + part_ref[r]
    total = total / FAN
    agg_ref[...] = total
    agg = jnp.concatenate([total[:, k * width : (k + 1) * width] for k in range(DST // 16)], axis=0)
    both = jnp.concatenate([own_ref[...].T, agg], axis=1)
    step = 256
    for at in range(0, hid, step):
        weight = jnp.concatenate([self_ref[:, at : at + step], neigh_ref[:, at : at + step]], axis=0)
        out_ref[:, at : at + step] = product(both, weight)


def project(part, own, w_self, w_neigh):
    return pl.pallas_call(
        project_kernel,
        in_specs=[VMEM] * 4,
        out_specs=[VMEM] * 2,
        out_shape=[
            jax.ShapeDtypeStruct(part.shape[1:], jnp.float32),
            jax.ShapeDtypeStruct((DST, w_self.shape[1]), jnp.float32),
        ],
        compiler_params=SMALL,
        name="project",
    )(part, own, w_self, w_neigh)


def gradient_kernel(pre_ref, grad_ref, own_ref, part_ref, hidden_ref, out_ref):
    width, hid = own_ref.shape[0], pre_ref.shape[1]
    turned = part_ref[...].T
    agg = jnp.concatenate([turned[k * width : (k + 1) * width] for k in range(DST // 16)], axis=1)
    lead, rest = split(jnp.concatenate([own_ref[...], agg], axis=0))
    both = jnp.concatenate([lead, rest], axis=0)
    step = 256
    for at in range(hid // step):
        value = pre_ref[:, at * step : (at + 1) * step]
        square = value * value
        bent = jnp.tanh(BEND * (value + CUBE * (value * square)))
        hidden_ref[:, at * step : (at + 1) * step] = (0.5 * value) * (1.0 + bent)
        slope = 0.5 * (1.0 + bent) + (0.5 * value) * (1.0 - bent * bent) * (BEND * (1.0 + (3.0 * CUBE) * square))
        high, low = split(grad_ref[:, at * step : (at + 1) * step] * slope)
        total = jnp.dot(both, high, preferred_element_type=jnp.float32)
        total = total[: 2 * width] + total[2 * width :] + jnp.dot(lead, low, preferred_element_type=jnp.float32)
        for line in range(4):
            for lane in range(step // 128):
                out_ref[line * (hid // 128) + at * (step // 128) + lane] = total[
                    line * 16 : line * 16 + 16, lane * 128 : lane * 128 + 128
                ]


def gradients(pre, grad_out, own, part):
    return pl.pallas_call(
        gradient_kernel,
        in_specs=[VMEM] * 4,
        out_specs=[VMEM] * 2,
        out_shape=[
            jax.ShapeDtypeStruct(pre.shape, jnp.float32),
            jax.ShapeDtypeStruct((N_ROW, 16, 128), jnp.float32),
        ],
        compiler_params=SMALL,
        name="gradients",
    )(pre, grad_out, own, part)


def spread_kernel(block_ref, self_ref, neigh_ref):
    lanes = self_ref.shape[1] // 128
    for at, out_ref in ((0, self_ref), (1, neigh_ref)):
        for line in range(2):
            for lane in range(lanes):
                out_ref[line * 16 : line * 16 + 16, lane * 128 : lane * 128 + 128] = block_ref[
                    (2 * at + line) * lanes + lane
                ]


def spread(blocks, hid):
    return pl.pallas_call(
        spread_kernel,
        in_specs=[VMEM],
        out_specs=[VMEM] * 2,
        out_shape=[jax.ShapeDtypeStruct((32, hid), jnp.float32)] * 2,
        compiler_params=SMALL,
        name="spread",
    )(blocks)


def body(features, dest_feat, owner, local_row, w_self, w_neigh, grad_out):
    hid = w_self.shape[1]
    asked = requests(owner.reshape(1, -1), local_row)
    asked = exchange(asked.reshape(N_ROW, 2, SLOTS), ACROSS).reshape(2 * N_ROW, SLOTS)
    core = lax.axis_index("core")
    own = dest_feat.T
    part = exchange(answers(asked, features, core.reshape(1)), ACROSS)
    agg, pre = project(part, own, w_self, w_neigh)
    pair = lax.all_gather(pre.reshape(2, DST // 2, hid), "core", axis=0, tiled=False)
    half = jnp.sum(lax.dynamic_index_in_dim(pair, core, axis=1, keepdims=False, allow_negative_indices=False), axis=0)
    half = half.reshape(3, 8, 4, 256).transpose(0, 2, 1, 3).reshape(N_Z, 8, 256)
    tile = jnp.sum(exchange(half, "z"), axis=0)
    half = exchange(jnp.broadcast_to(tile[None], (N_Z, 8, 256)), "z")
    half = half.reshape(3, 4, 8, 256).transpose(0, 2, 1, 3).reshape(DST // 2, hid)
    pre = lax.all_gather(half, "core", axis=0, tiled=True)
    hidden, part = gradients(pre, grad_out, own, agg)
    total = jnp.sum(exchange(part, ACROSS), axis=0)
    grads = exchange(jnp.broadcast_to(total[None], (N_ROW, 16, 128)), ACROSS)
    return (hidden, *spread(grads, hid))


def solution(mesh):
    grid = Mesh(mesh.devices.reshape(8, 4, 12, 2), ("y", "x", "z", "core"))
    return jax.shard_map(
        body,
        mesh=grid,
        in_specs=(P(ROW, COL), P(ROW, COL), P(ROW, None), P(ROW), P(COL, None), P(COL, None), P(ROW, None)),
        out_specs=(P(ROW, None), P(COL, None), P(COL, None)),
        check_vma=False,
    )
```

```python
import jax
import jax.numpy as jnp
from jax import lax
from jax.experimental import pallas as pl
from jax.experimental.pallas import tpu as pltpu
from jax.sharding import Mesh, PartitionSpec as P

FAN = 25
DST = 48
CAP = 75
ROOM = 80
SLOTS = 128
ROW = ("y", "x")
COL = ("z", "core")
N_ROW = 32
N_Z = 12
BEND = 0.7978845608
CUBE = 0.044715
LANES = (((1,), (1,)), ((), ()))
VMEM = pl.BlockSpec(memory_space=pltpu.VMEM)
ANY = pl.BlockSpec(memory_space=pl.ANY)
HBM = pl.BlockSpec(memory_space=pltpu.HBM)
SMALL = pltpu.CompilerParams(vmem_limit_bytes=16 << 20)


def exchange(value, axis):
    return lax.all_to_all(value, axis, split_axis=0, concat_axis=0, tiled=True)


def request_kernel(owner_from, row_from, out_ref, owner_ref, row_ref, sems):
    loads = [
        pltpu.make_async_copy(owner_from, owner_ref, sems.at[0]),
        pltpu.make_async_copy(row_from, row_ref, sems.at[1]),
    ]
    for load in loads:
        load.start()
    samples = owner_ref.shape[1]
    blocks = -(-samples // 128)
    line = lax.broadcasted_iota(jnp.int32, (2 * N_ROW, 128), 0)
    lane = lax.broadcasted_iota(jnp.int32, (1, 128), 1)
    even = (line & 1) == 0
    before = lax.broadcasted_iota(jnp.int32, (128, 128), 0) >= lax.broadcasted_iota(jnp.int32, (128, 128), 1)
    before = jnp.where(before, 1.0, 0.0).astype(jnp.bfloat16)
    slot = lax.broadcasted_iota(jnp.int32, (SLOTS, 128), 0).astype(jnp.float32)

    def padded(values, fill):
        width = values.shape[1]
        if width < 128:
            values = jnp.concatenate([values, jnp.full((1, 128 - width), fill, jnp.int32)], axis=1)
        return values

    for load in loads:
        load.wait()
    marks, counts = [], []
    for block in range(blocks):
        end = min(samples, block * 128 + 128)
        mark = padded(owner_ref[:, block * 128 : end], -1) == (line >> 1)
        marks.append(mark)
        counts.append(
            lax.dot_general(
                jnp.where(mark, 1.0, 0.0).astype(jnp.bfloat16), before, LANES, preferred_element_type=jnp.float32
            )
        )
    seen = jnp.full((2 * N_ROW, 1), -1.0, jnp.float32)
    lefts, rights = [], []
    for block in range(blocks):
        end = min(samples, block * 128 + 128)
        rows = padded(row_ref[block * 128 : end].reshape(1, -1), 0)
        mark, count = marks[block], counts[block]
        rank = jnp.sum(jnp.where(mark & even, count + seen, 0.0), axis=0, keepdims=True)
        seen = seen + count[:, 127:128]
        rights.append(jnp.where(rank == slot, 1.0, 0.0).astype(jnp.bfloat16))
        dest = (lane + block * 128) // FAN + 1
        high = jnp.where(mark, jnp.where(even, rows >> 6, dest), 0).astype(jnp.float32)
        low = jnp.where(mark & even, rows & 63, 0).astype(jnp.float32)
        lefts.append(jnp.concatenate([high, low], axis=0).astype(jnp.bfloat16))
    total = lax.dot_general(
        jnp.concatenate(lefts, axis=1), jnp.concatenate(rights, axis=1), LANES, preferred_element_type=jnp.float32
    )
    first, second = total[: 2 * N_ROW], total[2 * N_ROW :]
    out_ref[...] = (jnp.where(even, first * 64.0, first) + second).astype(jnp.int32)


def requests(owner, local_row):
    return pl.pallas_call(
        request_kernel,
        in_specs=[HBM, HBM],
        out_specs=VMEM,
        out_shape=jax.ShapeDtypeStruct((2 * N_ROW, SLOTS), jnp.int32),
        scratch_shapes=[
            pltpu.VMEM(owner.shape, jnp.int32),
            pltpu.VMEM(local_row.shape, jnp.int32),
            pltpu.SemaphoreType.DMA((2,)),
        ],
        name="requests",
    )(owner, local_row)


def answer_kernel(index_from, asked_ref, table_ref, core_ref, out_ref, held_ref, place_ref, index_ref, sem):
    width = table_ref.shape[1]
    load = pltpu.make_async_copy(index_from, index_ref, sem)
    load.start()
    line = lax.broadcasted_iota(jnp.int32, (DST, ROOM), 0) + 1
    for r in range(N_ROW):
        dest = asked_ref[2 * r + 1 : 2 * r + 2, :ROOM]
        place_ref[r] = jnp.where(dest == line, 1.0, 0.0).astype(jnp.bfloat16)
        held_ref[r, ROOM - 8 :, :] = jnp.zeros((8, width), jnp.float32)
    load.wait()

    def fetch(r, carry):
        for s in range(CAP):
            held_ref[r, s : s + 1, :] = table_ref[pl.ds(index_ref[r * CAP + s], 1), :]
        return carry

    lax.fori_loop(0, N_ROW, fetch, 0)
    gap = jnp.zeros((16, 128 - 3 * width), jnp.float32)
    for r in range(N_ROW):
        lead, rest = split(held_ref[r])
        total = jnp.dot(place_ref[r], jnp.concatenate([lead, rest], axis=1), preferred_element_type=jnp.float32)
        total = total[:, :width] + total[:, width:]
        out_ref[r] = jnp.concatenate([total[:16], total[16:32], total[32:], gap], axis=1)


def answers(asked, table, core):
    width = table.shape[1]
    index = asked.reshape(N_ROW, 2, SLOTS)[:, 0, :CAP].reshape(-1)
    return pl.pallas_call(
        answer_kernel,
        in_specs=[VMEM, VMEM, VMEM, ANY],
        out_specs=VMEM,
        out_shape=jax.ShapeDtypeStruct((N_ROW, 16, 128), jnp.float32),
        scratch_shapes=[
            pltpu.VMEM((N_ROW, ROOM, width), jnp.float32),
            pltpu.VMEM((N_ROW, DST, ROOM), jnp.bfloat16),
            pltpu.SMEM(index.shape, jnp.int32),
            pltpu.SemaphoreType.DMA,
        ],
        compiler_params=SMALL,
        name="answers",
    )(index, asked, table, core)


def split(value):
    lead = value.astype(jnp.bfloat16)
    return lead, (value - lead.astype(jnp.float32)).astype(jnp.bfloat16)


def product(left, right):
    lead, rest = split(left)
    high, low = split(right)
    total = jnp.dot(jnp.concatenate([lead, rest], axis=0), high, preferred_element_type=jnp.float32)
    lines = left.shape[0]
    return total[:lines] + total[lines:] + jnp.dot(lead, low, preferred_element_type=jnp.float32)


def project_kernel(part_ref, own_ref, self_ref, neigh_ref, agg_ref, out_ref):
    width, hid = self_ref.shape
    total = part_ref[0]
    for r in range(1, N_ROW):
        total = total + part_ref[r]
    total = total / FAN
    agg_ref[...] = total
    agg = jnp.concatenate([total[:, k * width : (k + 1) * width] for k in range(DST // 16)], axis=0)
    both = jnp.concatenate([own_ref[...].T, agg], axis=1)
    step = 256
    for at in range(0, hid, step):
        weight = jnp.concatenate([self_ref[:, at : at + step], neigh_ref[:, at : at + step]], axis=0)
        out_ref[:, at : at + step] = product(both, weight)


def project(part, own, w_self, w_neigh):
    return pl.pallas_call(
        project_kernel,
        in_specs=[VMEM] * 4,
        out_specs=[VMEM] * 2,
        out_shape=[
            jax.ShapeDtypeStruct(part.shape[1:], jnp.float32),
            jax.ShapeDtypeStruct((DST, w_self.shape[1]), jnp.float32),
        ],
        compiler_params=SMALL,
        name="project",
    )(part, own, w_self, w_neigh)


def gradient_kernel(pre_ref, grad_ref, own_ref, part_ref, hidden_ref, out_ref):
    width, hid = own_ref.shape[0], pre_ref.shape[1]
    turned = part_ref[...].T
    agg = jnp.concatenate([turned[k * width : (k + 1) * width] for k in range(DST // 16)], axis=1)
    lead, rest = split(jnp.concatenate([own_ref[...], agg], axis=0))
    both = jnp.concatenate([lead, rest], axis=0)
    step = 256
    for at in range(hid // step):
        value = pre_ref[:, at * step : (at + 1) * step]
        square = value * value
        bent = jnp.tanh(BEND * (value + CUBE * (value * square)))
        hidden_ref[:, at * step : (at + 1) * step] = (0.5 * value) * (1.0 + bent)
        slope = 0.5 * (1.0 + bent) + (0.5 * value) * (1.0 - bent * bent) * (BEND * (1.0 + (3.0 * CUBE) * square))
        high, low = split(grad_ref[:, at * step : (at + 1) * step] * slope)
        total = jnp.dot(both, high, preferred_element_type=jnp.float32)
        total = total[: 2 * width] + total[2 * width :] + jnp.dot(lead, low, preferred_element_type=jnp.float32)
        for line in range(4):
            for lane in range(step // 128):
                out_ref[line * (hid // 128) + at * (step // 128) + lane] = total[
                    line * 16 : line * 16 + 16, lane * 128 : lane * 128 + 128
                ]


def gradients(pre, grad_out, own, part):
    return pl.pallas_call(
        gradient_kernel,
        in_specs=[VMEM] * 4,
        out_specs=[VMEM] * 2,
        out_shape=[
            jax.ShapeDtypeStruct(pre.shape, jnp.float32),
            jax.ShapeDtypeStruct((N_ROW, 16, 128), jnp.float32),
        ],
        compiler_params=SMALL,
        name="gradients",
    )(pre, grad_out, own, part)


def spread_kernel(block_ref, hidden_ref, self_ref, neigh_ref, hidden_to, sem):
    store = pltpu.make_async_copy(hidden_ref, hidden_to, sem)
    store.start()
    lanes = self_ref.shape[1] // 128
    for at, out_ref in ((0, self_ref), (1, neigh_ref)):
        for line in range(2):
            for lane in range(lanes):
                out_ref[line * 16 : line * 16 + 16, lane * 128 : lane * 128 + 128] = block_ref[
                    (2 * at + line) * lanes + lane
                ]
    store.wait()


def spread(blocks, hidden):
    grad = jax.ShapeDtypeStruct((32, hidden.shape[1]), jnp.float32)
    return pl.pallas_call(
        spread_kernel,
        in_specs=[VMEM] * 2,
        out_specs=[VMEM, VMEM, HBM],
        out_shape=[grad, grad, jax.ShapeDtypeStruct(hidden.shape, jnp.float32)],
        scratch_shapes=[pltpu.SemaphoreType.DMA],
        compiler_params=SMALL,
        name="spread",
    )(blocks, hidden)


def body(features, dest_feat, owner, local_row, w_self, w_neigh, grad_out):
    hid = w_self.shape[1]
    asked = requests(owner.reshape(1, -1), local_row)
    asked = exchange(asked.reshape(N_ROW, 2, SLOTS), ROW).reshape(2 * N_ROW, SLOTS)
    core = lax.axis_index("core")
    own = dest_feat.T
    part = exchange(answers(asked, features, core.reshape(1)), ROW)
    agg, pre = project(part, own, w_self, w_neigh)
    pair = lax.all_gather(pre.reshape(2, DST // 2, hid), "core", axis=0, tiled=False)
    half = jnp.sum(lax.dynamic_index_in_dim(pair, core, axis=1, keepdims=False, allow_negative_indices=False), axis=0)
    half = half.reshape(3, 8, 4, 256).transpose(0, 2, 1, 3).reshape(N_Z, 8, 256)
    tile = jnp.sum(exchange(half, "z"), axis=0)
    half = exchange(jnp.broadcast_to(tile[None], (N_Z, 8, 256)), "z")
    half = half.reshape(3, 4, 8, 256).transpose(0, 2, 1, 3).reshape(DST // 2, hid)
    pre = lax.all_gather(half, "core", axis=0, tiled=True)
    hidden, part = gradients(pre, grad_out, own, agg)
    total = jnp.sum(exchange(part, ROW), axis=0)
    grads = exchange(jnp.broadcast_to(total[None], (N_ROW, 16, 128)), ROW)
    grad_self, grad_neigh, hidden = spread(grads, hidden)
    return (hidden, grad_self, grad_neigh)


def solution(mesh):
    grid = Mesh(mesh.devices.reshape(8, 4, 12, 2), ("y", "x", "z", "core"))
    return jax.shard_map(
        body,
        mesh=grid,
        in_specs=(P(ROW, COL), P(ROW, COL), P(ROW, None), P(ROW), P(COL, None), P(COL, None), P(ROW, None)),
        out_specs=(P(ROW, None), P(COL, None), P(COL, None)),
        check_vma=False,
    )
```

```python
import jax
import jax.numpy as jnp
from jax import lax
from jax.experimental import pallas as pl
from jax.experimental.pallas import tpu as pltpu
from jax.sharding import Mesh, PartitionSpec as P

FAN = 25
DST = 48
CAP = 75
ROOM = 80
SLOTS = 128
GROUP = 8
ROW = ("y", "x")
COL = ("z", "core")
N_ROW = 32
N_Z = 12
BEND = 0.7978845608
CUBE = 0.044715
LANES = (((1,), (1,)), ((), ()))
VMEM = pl.BlockSpec(memory_space=pltpu.VMEM)
ANY = pl.BlockSpec(memory_space=pl.ANY)
HBM = pl.BlockSpec(memory_space=pltpu.HBM)
SMALL = pltpu.CompilerParams(vmem_limit_bytes=16 << 20)


def exchange(value, axis):
    return lax.all_to_all(value, axis, split_axis=0, concat_axis=0, tiled=True)


def request_kernel(owner_from, row_from, out_ref, owner_ref, row_ref, sems):
    loads = [
        pltpu.make_async_copy(owner_from, owner_ref, sems.at[0]),
        pltpu.make_async_copy(row_from, row_ref, sems.at[1]),
    ]
    for load in loads:
        load.start()
    samples = owner_ref.shape[1]
    blocks = -(-samples // 128)
    line = lax.broadcasted_iota(jnp.int32, (2 * N_ROW, 128), 0)
    lane = lax.broadcasted_iota(jnp.int32, (1, 128), 1)
    even = (line & 1) == 0
    before = lax.broadcasted_iota(jnp.int32, (128, 128), 0) >= lax.broadcasted_iota(jnp.int32, (128, 128), 1)
    before = jnp.where(before, 1.0, 0.0).astype(jnp.bfloat16)
    slot = lax.broadcasted_iota(jnp.int32, (SLOTS, 128), 0).astype(jnp.float32)

    def padded(values, fill):
        width = values.shape[1]
        if width < 128:
            values = jnp.concatenate([values, jnp.full((1, 128 - width), fill, jnp.int32)], axis=1)
        return values

    for load in loads:
        load.wait()
    marks, counts = [], []
    for block in range(blocks):
        end = min(samples, block * 128 + 128)
        mark = padded(owner_ref[:, block * 128 : end], -1) == (line >> 1)
        marks.append(mark)
        counts.append(
            lax.dot_general(
                jnp.where(mark, 1.0, 0.0).astype(jnp.bfloat16), before, LANES, preferred_element_type=jnp.float32
            )
        )
    seen = jnp.full((2 * N_ROW, 1), -1.0, jnp.float32)
    lefts, rights = [], []
    for block in range(blocks):
        end = min(samples, block * 128 + 128)
        rows = padded(row_ref[block * 128 : end].reshape(1, -1), 0)
        mark, count = marks[block], counts[block]
        rank = jnp.sum(jnp.where(mark & even, count + seen, 0.0), axis=0, keepdims=True)
        seen = seen + count[:, 127:128]
        rights.append(jnp.where(rank == slot, 1.0, 0.0).astype(jnp.bfloat16))
        dest = (lane + block * 128) // FAN + 1
        high = jnp.where(mark, jnp.where(even, rows >> 6, dest), 0).astype(jnp.float32)
        low = jnp.where(mark & even, rows & 63, 0).astype(jnp.float32)
        lefts.append(jnp.concatenate([high, low], axis=0).astype(jnp.bfloat16))
    total = lax.dot_general(
        jnp.concatenate(lefts, axis=1), jnp.concatenate(rights, axis=1), LANES, preferred_element_type=jnp.float32
    )
    first, second = total[: 2 * N_ROW], total[2 * N_ROW :]
    out_ref[...] = (jnp.where(even, first * 64.0, first) + second).astype(jnp.int32)


def requests(owner, local_row):
    return pl.pallas_call(
        request_kernel,
        in_specs=[HBM, HBM],
        out_specs=VMEM,
        out_shape=jax.ShapeDtypeStruct((2 * N_ROW, SLOTS), jnp.int32),
        scratch_shapes=[
            pltpu.VMEM(owner.shape, jnp.int32),
            pltpu.VMEM(local_row.shape, jnp.int32),
            pltpu.SemaphoreType.DMA((2,)),
        ],
        name="requests",
    )(owner, local_row)


def answer_kernel(index_from, asked_ref, table_ref, core_ref, out_ref, held_ref, place_ref, index_ref, sem):
    width = table_ref.shape[1]
    load = pltpu.make_async_copy(index_from, index_ref, sem)
    load.start()
    line = lax.broadcasted_iota(jnp.int32, (DST, ROOM), 0) + 1
    for r in range(N_ROW):
        dest = asked_ref[2 * r + 1 : 2 * r + 2, :ROOM]
        place_ref[r] = jnp.where(dest == line, 1.0, 0.0).astype(jnp.bfloat16)
        held_ref[r, ROOM - 8 :, :] = jnp.zeros((8, width), jnp.float32)
    load.wait()
    gap = jnp.zeros((16, 128 - 3 * width), jnp.float32)

    def fetch(r, s):
        held_ref[r, s : s + 1, :] = table_ref[pl.ds(index_ref[r * CAP + s], 1), :]

    def reply(r):
        lead, rest = split(held_ref[r])
        total = jnp.dot(place_ref[r], jnp.concatenate([lead, rest], axis=1), preferred_element_type=jnp.float32)
        total = total[:, :width] + total[:, width:]
        out_ref[r] = jnp.concatenate([total[:16], total[16:32], total[32:], gap], axis=1)

    for r in range(N_ROW + GROUP):
        if r >= GROUP:
            reply(r - GROUP)
        if r < N_ROW:
            for s in range(CAP):
                fetch(r, s)


def answers(asked, table, core):
    width = table.shape[1]
    index = asked.reshape(N_ROW, 2, SLOTS)[:, 0, :CAP].reshape(-1)
    return pl.pallas_call(
        answer_kernel,
        in_specs=[VMEM, VMEM, VMEM, ANY],
        out_specs=VMEM,
        out_shape=jax.ShapeDtypeStruct((N_ROW, 16, 128), jnp.float32),
        scratch_shapes=[
            pltpu.VMEM((N_ROW, ROOM, width), jnp.float32),
            pltpu.VMEM((N_ROW, DST, ROOM), jnp.bfloat16),
            pltpu.SMEM(index.shape, jnp.int32),
            pltpu.SemaphoreType.DMA,
        ],
        compiler_params=SMALL,
        name="answers",
    )(index, asked, table, core)


def split(value):
    lead = value.astype(jnp.bfloat16)
    return lead, (value - lead.astype(jnp.float32)).astype(jnp.bfloat16)


def product(left, right):
    lead, rest = split(left)
    high, low = split(right)
    total = jnp.dot(jnp.concatenate([lead, rest], axis=0), high, preferred_element_type=jnp.float32)
    lines = left.shape[0]
    return total[:lines] + total[lines:] + jnp.dot(lead, low, preferred_element_type=jnp.float32)


def project_kernel(part_ref, own_ref, self_ref, neigh_ref, agg_ref, out_ref):
    width, hid = self_ref.shape
    total = part_ref[0]
    for r in range(1, N_ROW):
        total = total + part_ref[r]
    total = total / FAN
    agg_ref[...] = total
    agg = jnp.concatenate([total[:, k * width : (k + 1) * width] for k in range(DST // 16)], axis=0)
    both = jnp.concatenate([own_ref[...].T, agg], axis=1)
    step = 256
    for at in range(0, hid, step):
        weight = jnp.concatenate([self_ref[:, at : at + step], neigh_ref[:, at : at + step]], axis=0)
        out_ref[:, at : at + step] = product(both, weight)


def project(part, own, w_self, w_neigh):
    return pl.pallas_call(
        project_kernel,
        in_specs=[VMEM] * 4,
        out_specs=[VMEM] * 2,
        out_shape=[
            jax.ShapeDtypeStruct(part.shape[1:], jnp.float32),
            jax.ShapeDtypeStruct((DST, w_self.shape[1]), jnp.float32),
        ],
        compiler_params=SMALL,
        name="project",
    )(part, own, w_self, w_neigh)


def gradient_kernel(pre_ref, grad_ref, own_ref, part_ref, hidden_ref, out_ref):
    width, hid = own_ref.shape[0], pre_ref.shape[1]
    turned = part_ref[...].T
    agg = jnp.concatenate([turned[k * width : (k + 1) * width] for k in range(DST // 16)], axis=1)
    lead, rest = split(jnp.concatenate([own_ref[...], agg], axis=0))
    both = jnp.concatenate([lead, rest], axis=0)
    step = 256
    for at in range(hid // step):
        value = pre_ref[:, at * step : (at + 1) * step]
        square = value * value
        bent = jnp.tanh(BEND * (value + CUBE * (value * square)))
        hidden_ref[:, at * step : (at + 1) * step] = (0.5 * value) * (1.0 + bent)
        slope = 0.5 * (1.0 + bent) + (0.5 * value) * (1.0 - bent * bent) * (BEND * (1.0 + (3.0 * CUBE) * square))
        high, low = split(grad_ref[:, at * step : (at + 1) * step] * slope)
        total = jnp.dot(both, high, preferred_element_type=jnp.float32)
        total = total[: 2 * width] + total[2 * width :] + jnp.dot(lead, low, preferred_element_type=jnp.float32)
        for line in range(4):
            for lane in range(step // 128):
                out_ref[line * (hid // 128) + at * (step // 128) + lane] = total[
                    line * 16 : line * 16 + 16, lane * 128 : lane * 128 + 128
                ]


def gradients(pre, grad_out, own, part):
    return pl.pallas_call(
        gradient_kernel,
        in_specs=[VMEM] * 4,
        out_specs=[VMEM] * 2,
        out_shape=[
            jax.ShapeDtypeStruct(pre.shape, jnp.float32),
            jax.ShapeDtypeStruct((N_ROW, 16, 128), jnp.float32),
        ],
        compiler_params=SMALL,
        name="gradients",
    )(pre, grad_out, own, part)


def spread_kernel(block_ref, self_ref, neigh_ref):
    lanes = self_ref.shape[1] // 128
    for at, out_ref in ((0, self_ref), (1, neigh_ref)):
        for line in range(2):
            for lane in range(lanes):
                out_ref[line * 16 : line * 16 + 16, lane * 128 : lane * 128 + 128] = block_ref[
                    (2 * at + line) * lanes + lane
                ]


def spread(blocks, hid):
    return pl.pallas_call(
        spread_kernel,
        in_specs=[VMEM],
        out_specs=[VMEM] * 2,
        out_shape=[jax.ShapeDtypeStruct((32, hid), jnp.float32)] * 2,
        compiler_params=SMALL,
        name="spread",
    )(blocks)


def body(features, dest_feat, owner, local_row, w_self, w_neigh, grad_out):
    hid = w_self.shape[1]
    asked = requests(owner.reshape(1, -1), local_row)
    asked = exchange(asked.reshape(N_ROW, 2, SLOTS), ROW).reshape(2 * N_ROW, SLOTS)
    core = lax.axis_index("core")
    own = dest_feat.T
    part = exchange(answers(asked, features, core.reshape(1)), ROW)
    agg, pre = project(part, own, w_self, w_neigh)
    pair = lax.all_gather(pre.reshape(2, DST // 2, hid), "core", axis=0, tiled=False)
    half = jnp.sum(lax.dynamic_index_in_dim(pair, core, axis=1, keepdims=False, allow_negative_indices=False), axis=0)
    half = half.reshape(3, 8, 4, 256).transpose(0, 2, 1, 3).reshape(N_Z, 8, 256)
    tile = jnp.sum(exchange(half, "z"), axis=0)
    half = exchange(jnp.broadcast_to(tile[None], (N_Z, 8, 256)), "z")
    half = half.reshape(3, 4, 8, 256).transpose(0, 2, 1, 3).reshape(DST // 2, hid)
    pre = lax.all_gather(half, "core", axis=0, tiled=True)
    hidden, part = gradients(pre, grad_out, own, agg)
    total = jnp.sum(exchange(part, ROW), axis=0)
    grads = exchange(jnp.broadcast_to(total[None], (N_ROW, 16, 128)), ROW)
    return (hidden, *spread(grads, hid))


def solution(mesh):
    grid = Mesh(mesh.devices.reshape(8, 4, 12, 2), ("y", "x", "z", "core"))
    return jax.shard_map(
        body,
        mesh=grid,
        in_specs=(P(ROW, COL), P(ROW, COL), P(ROW, None), P(ROW), P(COL, None), P(COL, None), P(ROW, None)),
        out_specs=(P(ROW, None), P(COL, None), P(COL, None)),
        check_vma=False,
    )
```

```python
import jax
import jax.numpy as jnp
from jax import lax
from jax.experimental import pallas as pl
from jax.experimental.pallas import tpu as pltpu
from jax.sharding import Mesh, PartitionSpec as P

FAN = 25
DST = 48
CAP = 75
ROOM = 80
SLOTS = 128
GROUP = 8
ROW = ("y", "x")
ACROSS = ("x", "y")
COL = ("z", "core")
N_ROW = 32
N_Z = 12
BEND = 0.7978845608
CUBE = 0.044715
LANES = (((1,), (1,)), ((), ()))
VMEM = pl.BlockSpec(memory_space=pltpu.VMEM)
ANY = pl.BlockSpec(memory_space=pl.ANY)
HBM = pl.BlockSpec(memory_space=pltpu.HBM)
SMALL = pltpu.CompilerParams(vmem_limit_bytes=16 << 20)


def exchange(value, axis):
    return lax.all_to_all(value, axis, split_axis=0, concat_axis=0, tiled=True)


def request_kernel(owner_from, row_from, out_ref, owner_ref, row_ref, sems):
    loads = [
        pltpu.make_async_copy(owner_from, owner_ref, sems.at[0]),
        pltpu.make_async_copy(row_from, row_ref, sems.at[1]),
    ]
    for load in loads:
        load.start()
    samples = owner_ref.shape[1]
    blocks = -(-samples // 128)
    line = lax.broadcasted_iota(jnp.int32, (2 * N_ROW, 128), 0)
    lane = lax.broadcasted_iota(jnp.int32, (1, 128), 1)
    even = (line & 1) == 0
    before = lax.broadcasted_iota(jnp.int32, (128, 128), 0) >= lax.broadcasted_iota(jnp.int32, (128, 128), 1)
    before = jnp.where(before, 1.0, 0.0).astype(jnp.bfloat16)
    slot = lax.broadcasted_iota(jnp.int32, (SLOTS, 128), 0).astype(jnp.float32)

    def padded(values, fill):
        width = values.shape[1]
        if width < 128:
            values = jnp.concatenate([values, jnp.full((1, 128 - width), fill, jnp.int32)], axis=1)
        return values

    for load in loads:
        load.wait()
    marks, counts = [], []
    for block in range(blocks):
        end = min(samples, block * 128 + 128)
        owners = padded(owner_ref[:, block * 128 : end], -1)
        mark = ((owners & 3) * 8 + (owners >> 2)) == (line >> 1)
        marks.append(mark)
        counts.append(
            lax.dot_general(
                jnp.where(mark, 1.0, 0.0).astype(jnp.bfloat16), before, LANES, preferred_element_type=jnp.float32
            )
        )
    seen = jnp.full((2 * N_ROW, 1), -1.0, jnp.float32)
    lefts, rights = [], []
    for block in range(blocks):
        end = min(samples, block * 128 + 128)
        rows = padded(row_ref[block * 128 : end].reshape(1, -1), 0)
        mark, count = marks[block], counts[block]
        rank = jnp.sum(jnp.where(mark & even, count + seen, 0.0), axis=0, keepdims=True)
        seen = seen + count[:, 127:128]
        rights.append(jnp.where(rank == slot, 1.0, 0.0).astype(jnp.bfloat16))
        dest = (lane + block * 128) // FAN + 1
        high = jnp.where(mark, jnp.where(even, rows >> 6, dest), 0).astype(jnp.float32)
        low = jnp.where(mark & even, rows & 63, 0).astype(jnp.float32)
        lefts.append(jnp.concatenate([high, low], axis=0).astype(jnp.bfloat16))
    total = lax.dot_general(
        jnp.concatenate(lefts, axis=1), jnp.concatenate(rights, axis=1), LANES, preferred_element_type=jnp.float32
    )
    first, second = total[: 2 * N_ROW], total[2 * N_ROW :]
    out_ref[...] = (jnp.where(even, first * 64.0, first) + second).astype(jnp.int32)


def requests(owner, local_row):
    return pl.pallas_call(
        request_kernel,
        in_specs=[HBM, HBM],
        out_specs=VMEM,
        out_shape=jax.ShapeDtypeStruct((2 * N_ROW, SLOTS), jnp.int32),
        scratch_shapes=[
            pltpu.VMEM(owner.shape, jnp.int32),
            pltpu.VMEM(local_row.shape, jnp.int32),
            pltpu.SemaphoreType.DMA((2,)),
        ],
        name="requests",
    )(owner, local_row)


def answer_kernel(index_from, asked_ref, table_ref, core_ref, out_ref, held_ref, place_ref, index_ref, sem):
    width = table_ref.shape[1]
    load = pltpu.make_async_copy(index_from, index_ref, sem)
    load.start()
    line = lax.broadcasted_iota(jnp.int32, (DST, ROOM), 0) + 1
    for r in range(N_ROW):
        dest = asked_ref[2 * r + 1 : 2 * r + 2, :ROOM]
        place_ref[r] = jnp.where(dest == line, 1.0, 0.0).astype(jnp.bfloat16)
        held_ref[r, ROOM - 8 :, :] = jnp.zeros((8, width), jnp.float32)
    load.wait()
    gap = jnp.zeros((16, 128 - 3 * width), jnp.float32)

    def fetch(r, s):
        held_ref[r, s : s + 1, :] = table_ref[pl.ds(index_ref[r * CAP + s], 1), :]

    def reply(r):
        lead, rest = split(held_ref[r])
        total = jnp.dot(place_ref[r], jnp.concatenate([lead, rest], axis=1), preferred_element_type=jnp.float32)
        total = total[:, :width] + total[:, width:]
        out_ref[r] = jnp.concatenate([total[:16], total[16:32], total[32:], gap], axis=1)

    for r in range(N_ROW + GROUP):
        if r >= GROUP:
            reply(r - GROUP)
        if r < N_ROW:
            for s in range(CAP):
                fetch(r, s)


def answers(asked, table, core):
    width = table.shape[1]
    index = asked.reshape(N_ROW, 2, SLOTS)[:, 0, :CAP].reshape(-1)
    return pl.pallas_call(
        answer_kernel,
        in_specs=[VMEM, VMEM, VMEM, ANY],
        out_specs=VMEM,
        out_shape=jax.ShapeDtypeStruct((N_ROW, 16, 128), jnp.float32),
        scratch_shapes=[
            pltpu.VMEM((N_ROW, ROOM, width), jnp.float32),
            pltpu.VMEM((N_ROW, DST, ROOM), jnp.bfloat16),
            pltpu.SMEM(index.shape, jnp.int32),
            pltpu.SemaphoreType.DMA,
        ],
        compiler_params=SMALL,
        name="answers",
    )(index, asked, table, core)


def split(value):
    lead = value.astype(jnp.bfloat16)
    return lead, (value - lead.astype(jnp.float32)).astype(jnp.bfloat16)


def product(left, right):
    lead, rest = split(left)
    high, low = split(right)
    total = jnp.dot(jnp.concatenate([lead, rest], axis=0), high, preferred_element_type=jnp.float32)
    lines = left.shape[0]
    return total[:lines] + total[lines:] + jnp.dot(lead, low, preferred_element_type=jnp.float32)


def project_kernel(part_ref, own_ref, self_ref, neigh_ref, agg_ref, out_ref):
    width, hid = self_ref.shape
    total = part_ref[0]
    for r in range(1, N_ROW):
        total = total + part_ref[r]
    total = total / FAN
    agg_ref[...] = total
    agg = jnp.concatenate([total[:, k * width : (k + 1) * width] for k in range(DST // 16)], axis=0)
    both = jnp.concatenate([own_ref[...].T, agg], axis=1)
    step = 256
    for at in range(0, hid, step):
        weight = jnp.concatenate([self_ref[:, at : at + step], neigh_ref[:, at : at + step]], axis=0)
        out_ref[:, at : at + step] = product(both, weight)


def project(part, own, w_self, w_neigh):
    return pl.pallas_call(
        project_kernel,
        in_specs=[VMEM] * 4,
        out_specs=[VMEM] * 2,
        out_shape=[
            jax.ShapeDtypeStruct(part.shape[1:], jnp.float32),
            jax.ShapeDtypeStruct((DST, w_self.shape[1]), jnp.float32),
        ],
        compiler_params=SMALL,
        name="project",
    )(part, own, w_self, w_neigh)


def gradient_kernel(pre_ref, grad_ref, own_ref, part_ref, hidden_ref, out_ref):
    width, hid = own_ref.shape[0], pre_ref.shape[1]
    turned = part_ref[...].T
    agg = jnp.concatenate([turned[k * width : (k + 1) * width] for k in range(DST // 16)], axis=1)
    lead, rest = split(jnp.concatenate([own_ref[...], agg], axis=0))
    both = jnp.concatenate([lead, rest], axis=0)
    step = 256
    for at in range(hid // step):
        value = pre_ref[:, at * step : (at + 1) * step]
        square = value * value
        bent = jnp.tanh(BEND * (value + CUBE * (value * square)))
        hidden_ref[:, at * step : (at + 1) * step] = (0.5 * value) * (1.0 + bent)
        slope = 0.5 * (1.0 + bent) + (0.5 * value) * (1.0 - bent * bent) * (BEND * (1.0 + (3.0 * CUBE) * square))
        high, low = split(grad_ref[:, at * step : (at + 1) * step] * slope)
        total = jnp.dot(both, high, preferred_element_type=jnp.float32)
        total = total[: 2 * width] + total[2 * width :] + jnp.dot(lead, low, preferred_element_type=jnp.float32)
        for line in range(4):
            for lane in range(step // 128):
                out_ref[line * (hid // 128) + at * (step // 128) + lane] = total[
                    line * 16 : line * 16 + 16, lane * 128 : lane * 128 + 128
                ]


def gradients(pre, grad_out, own, part):
    return pl.pallas_call(
        gradient_kernel,
        in_specs=[VMEM] * 4,
        out_specs=[VMEM] * 2,
        out_shape=[
            jax.ShapeDtypeStruct(pre.shape, jnp.float32),
            jax.ShapeDtypeStruct((N_ROW, 16, 128), jnp.float32),
        ],
        compiler_params=SMALL,
        name="gradients",
    )(pre, grad_out, own, part)


def spread_kernel(block_ref, self_ref, neigh_ref):
    lanes = self_ref.shape[1] // 128
    for at, out_ref in ((0, self_ref), (1, neigh_ref)):
        for line in range(2):
            for lane in range(lanes):
                out_ref[line * 16 : line * 16 + 16, lane * 128 : lane * 128 + 128] = block_ref[
                    (2 * at + line) * lanes + lane
                ]


def spread(blocks, hid):
    return pl.pallas_call(
        spread_kernel,
        in_specs=[VMEM],
        out_specs=[VMEM] * 2,
        out_shape=[jax.ShapeDtypeStruct((32, hid), jnp.float32)] * 2,
        compiler_params=SMALL,
        name="spread",
    )(blocks)


def body(features, dest_feat, owner, local_row, w_self, w_neigh, grad_out):
    hid = w_self.shape[1]
    asked = requests(owner.reshape(1, -1), local_row)
    asked = exchange(asked.reshape(N_ROW, 2, SLOTS), ACROSS).reshape(2 * N_ROW, SLOTS)
    core = lax.axis_index("core")
    own = dest_feat.T
    part = exchange(answers(asked, features, core.reshape(1)), ACROSS)
    agg, pre = project(part, own, w_self, w_neigh)
    pair = lax.all_gather(pre.reshape(2, DST // 2, hid), "core", axis=0, tiled=False)
    half = jnp.sum(lax.dynamic_index_in_dim(pair, core, axis=1, keepdims=False, allow_negative_indices=False), axis=0)
    half = half.reshape(3, 8, 4, 256).transpose(0, 2, 1, 3).reshape(N_Z, 8, 256)
    tile = jnp.sum(exchange(half, "z"), axis=0)
    half = exchange(jnp.broadcast_to(tile[None], (N_Z, 8, 256)), "z")
    half = half.reshape(3, 4, 8, 256).transpose(0, 2, 1, 3).reshape(DST // 2, hid)
    pre = lax.all_gather(half, "core", axis=0, tiled=True)
    hidden, part = gradients(pre, grad_out, own, agg)
    total = jnp.sum(exchange(part, ROW), axis=0)
    grads = exchange(jnp.broadcast_to(total[None], (N_ROW, 16, 128)), ROW)
    return (hidden, *spread(grads, hid))


def solution(mesh):
    grid = Mesh(mesh.devices.reshape(8, 4, 12, 2), ("y", "x", "z", "core"))
    return jax.shard_map(
        body,
        mesh=grid,
        in_specs=(P(ROW, COL), P(ROW, COL), P(ROW, None), P(ROW), P(COL, None), P(COL, None), P(ROW, None)),
        out_specs=(P(ROW, None), P(COL, None), P(COL, None)),
        check_vma=False,
    )
```

```python
import jax
import jax.numpy as jnp
from jax import lax
from jax.experimental import pallas as pl
from jax.experimental.pallas import tpu as pltpu
from jax.sharding import Mesh, PartitionSpec as P

FAN = 25
DST = 48
CAP = 75
ROOM = 80
SLOTS = 128
GROUP = 4
ROW = ("y", "x")
COL = ("z", "core")
N_ROW = 32
N_Z = 12
BEND = 0.7978845608
CUBE = 0.044715
LANES = (((1,), (1,)), ((), ()))
VMEM = pl.BlockSpec(memory_space=pltpu.VMEM)
ANY = pl.BlockSpec(memory_space=pl.ANY)
HBM = pl.BlockSpec(memory_space=pltpu.HBM)
SMALL = pltpu.CompilerParams(vmem_limit_bytes=16 << 20)


def exchange(value, axis):
    return lax.all_to_all(value, axis, split_axis=0, concat_axis=0, tiled=True)


def request_kernel(owner_from, row_from, out_ref, owner_ref, row_ref, sems):
    loads = [
        pltpu.make_async_copy(owner_from, owner_ref, sems.at[0]),
        pltpu.make_async_copy(row_from, row_ref, sems.at[1]),
    ]
    for load in loads:
        load.start()
    samples = owner_ref.shape[1]
    blocks = -(-samples // 128)
    line = lax.broadcasted_iota(jnp.int32, (2 * N_ROW, 128), 0)
    lane = lax.broadcasted_iota(jnp.int32, (1, 128), 1)
    even = (line & 1) == 0
    before = lax.broadcasted_iota(jnp.int32, (128, 128), 0) >= lax.broadcasted_iota(jnp.int32, (128, 128), 1)
    before = jnp.where(before, 1.0, 0.0).astype(jnp.bfloat16)
    slot = lax.broadcasted_iota(jnp.int32, (SLOTS, 128), 0).astype(jnp.float32)

    def padded(values, fill):
        width = values.shape[1]
        if width < 128:
            values = jnp.concatenate([values, jnp.full((1, 128 - width), fill, jnp.int32)], axis=1)
        return values

    for load in loads:
        load.wait()
    marks, counts = [], []
    for block in range(blocks):
        end = min(samples, block * 128 + 128)
        mark = padded(owner_ref[:, block * 128 : end], -1) == (line >> 1)
        marks.append(mark)
        counts.append(
            lax.dot_general(
                jnp.where(mark, 1.0, 0.0).astype(jnp.bfloat16), before, LANES, preferred_element_type=jnp.float32
            )
        )
    seen = jnp.full((2 * N_ROW, 1), -1.0, jnp.float32)
    lefts, rights = [], []
    for block in range(blocks):
        end = min(samples, block * 128 + 128)
        rows = padded(row_ref[block * 128 : end].reshape(1, -1), 0)
        mark, count = marks[block], counts[block]
        rank = jnp.sum(jnp.where(mark & even, count + seen, 0.0), axis=0, keepdims=True)
        seen = seen + count[:, 127:128]
        rights.append(jnp.where(rank == slot, 1.0, 0.0).astype(jnp.bfloat16))
        dest = (lane + block * 128) // FAN + 1
        high = jnp.where(mark, jnp.where(even, rows >> 6, dest), 0).astype(jnp.float32)
        low = jnp.where(mark & even, rows & 63, 0).astype(jnp.float32)
        lefts.append(jnp.concatenate([high, low], axis=0).astype(jnp.bfloat16))
    total = lax.dot_general(
        jnp.concatenate(lefts, axis=1), jnp.concatenate(rights, axis=1), LANES, preferred_element_type=jnp.float32
    )
    first, second = total[: 2 * N_ROW], total[2 * N_ROW :]
    out_ref[...] = (jnp.where(even, first * 64.0, first) + second).astype(jnp.int32)


def requests(owner, local_row):
    return pl.pallas_call(
        request_kernel,
        in_specs=[HBM, HBM],
        out_specs=VMEM,
        out_shape=jax.ShapeDtypeStruct((2 * N_ROW, SLOTS), jnp.int32),
        scratch_shapes=[
            pltpu.VMEM(owner.shape, jnp.int32),
            pltpu.VMEM(local_row.shape, jnp.int32),
            pltpu.SemaphoreType.DMA((2,)),
        ],
        name="requests",
    )(owner, local_row)


def answer_kernel(index_from, asked_ref, table_ref, core_ref, out_ref, held_ref, place_ref, index_ref, sem):
    width = table_ref.shape[1]
    load = pltpu.make_async_copy(index_from, index_ref, sem)
    load.start()
    line = lax.broadcasted_iota(jnp.int32, (DST, ROOM), 0) + 1
    for r in range(N_ROW):
        dest = asked_ref[2 * r + 1 : 2 * r + 2, :ROOM]
        place_ref[r] = jnp.where(dest == line, 1.0, 0.0).astype(jnp.bfloat16)
        held_ref[r, ROOM - 8 :, :] = jnp.zeros((8, width), jnp.float32)
    load.wait()
    gap = jnp.zeros((16, 128 - 3 * width), jnp.float32)

    def fetch(r, s):
        held_ref[r, s : s + 1, :] = table_ref[pl.ds(index_ref[r * CAP + s], 1), :]

    def reply(r):
        lead, rest = split(held_ref[r])
        total = jnp.dot(place_ref[r], jnp.concatenate([lead, rest], axis=1), preferred_element_type=jnp.float32)
        total = total[:, :width] + total[:, width:]
        out_ref[r] = jnp.concatenate([total[:16], total[16:32], total[32:], gap], axis=1)

    for r in range(N_ROW + GROUP):
        if r >= GROUP:
            reply(r - GROUP)
        if r < N_ROW:
            for s in range(CAP):
                fetch(r, s)


def answers(asked, table, core):
    width = table.shape[1]
    index = asked.reshape(N_ROW, 2, SLOTS)[:, 0, :CAP].reshape(-1)
    return pl.pallas_call(
        answer_kernel,
        in_specs=[VMEM, VMEM, VMEM, ANY],
        out_specs=VMEM,
        out_shape=jax.ShapeDtypeStruct((N_ROW, 16, 128), jnp.float32),
        scratch_shapes=[
            pltpu.VMEM((N_ROW, ROOM, width), jnp.float32),
            pltpu.VMEM((N_ROW, DST, ROOM), jnp.bfloat16),
            pltpu.SMEM(index.shape, jnp.int32),
            pltpu.SemaphoreType.DMA,
        ],
        compiler_params=SMALL,
        name="answers",
    )(index, asked, table, core)


def split(value):
    lead = value.astype(jnp.bfloat16)
    return lead, (value - lead.astype(jnp.float32)).astype(jnp.bfloat16)


def product(left, right):
    lead, rest = split(left)
    high, low = split(right)
    total = jnp.dot(jnp.concatenate([lead, rest], axis=0), high, preferred_element_type=jnp.float32)
    lines = left.shape[0]
    return total[:lines] + total[lines:] + jnp.dot(lead, low, preferred_element_type=jnp.float32)


def project_kernel(part_ref, own_ref, self_ref, neigh_ref, agg_ref, out_ref):
    width, hid = self_ref.shape
    total = part_ref[0]
    for r in range(1, N_ROW):
        total = total + part_ref[r]
    total = total / FAN
    agg_ref[...] = total
    agg = jnp.concatenate([total[:, k * width : (k + 1) * width] for k in range(DST // 16)], axis=0)
    both = jnp.concatenate([own_ref[...].T, agg], axis=1)
    step = 256
    for at in range(0, hid, step):
        weight = jnp.concatenate([self_ref[:, at : at + step], neigh_ref[:, at : at + step]], axis=0)
        out_ref[:, at : at + step] = product(both, weight)


def project(part, own, w_self, w_neigh):
    return pl.pallas_call(
        project_kernel,
        in_specs=[VMEM] * 4,
        out_specs=[VMEM] * 2,
        out_shape=[
            jax.ShapeDtypeStruct(part.shape[1:], jnp.float32),
            jax.ShapeDtypeStruct((DST, w_self.shape[1]), jnp.float32),
        ],
        compiler_params=SMALL,
        name="project",
    )(part, own, w_self, w_neigh)


def gradient_kernel(pre_ref, grad_ref, own_ref, part_ref, hidden_ref, out_ref):
    width, hid = own_ref.shape[0], pre_ref.shape[1]
    turned = part_ref[...].T
    agg = jnp.concatenate([turned[k * width : (k + 1) * width] for k in range(DST // 16)], axis=1)
    lead, rest = split(jnp.concatenate([own_ref[...], agg], axis=0))
    both = jnp.concatenate([lead, rest], axis=0)
    step = 256
    for at in range(hid // step):
        value = pre_ref[:, at * step : (at + 1) * step]
        square = value * value
        bent = jnp.tanh(BEND * (value + CUBE * (value * square)))
        hidden_ref[:, at * step : (at + 1) * step] = (0.5 * value) * (1.0 + bent)
        slope = 0.5 * (1.0 + bent) + (0.5 * value) * (1.0 - bent * bent) * (BEND * (1.0 + (3.0 * CUBE) * square))
        high, low = split(grad_ref[:, at * step : (at + 1) * step] * slope)
        total = jnp.dot(both, high, preferred_element_type=jnp.float32)
        total = total[: 2 * width] + total[2 * width :] + jnp.dot(lead, low, preferred_element_type=jnp.float32)
        for line in range(4):
            for lane in range(step // 128):
                out_ref[line * (hid // 128) + at * (step // 128) + lane] = total[
                    line * 16 : line * 16 + 16, lane * 128 : lane * 128 + 128
                ]


def gradients(pre, grad_out, own, part):
    return pl.pallas_call(
        gradient_kernel,
        in_specs=[VMEM] * 4,
        out_specs=[VMEM] * 2,
        out_shape=[
            jax.ShapeDtypeStruct(pre.shape, jnp.float32),
            jax.ShapeDtypeStruct((N_ROW, 16, 128), jnp.float32),
        ],
        compiler_params=SMALL,
        name="gradients",
    )(pre, grad_out, own, part)


def spread_kernel(block_ref, self_ref, neigh_ref):
    lanes = self_ref.shape[1] // 128
    for at, out_ref in ((0, self_ref), (1, neigh_ref)):
        for line in range(2):
            for lane in range(lanes):
                out_ref[line * 16 : line * 16 + 16, lane * 128 : lane * 128 + 128] = block_ref[
                    (2 * at + line) * lanes + lane
                ]


def spread(blocks, hid):
    return pl.pallas_call(
        spread_kernel,
        in_specs=[VMEM],
        out_specs=[VMEM] * 2,
        out_shape=[jax.ShapeDtypeStruct((32, hid), jnp.float32)] * 2,
        compiler_params=SMALL,
        name="spread",
    )(blocks)


def body(features, dest_feat, owner, local_row, w_self, w_neigh, grad_out):
    hid = w_self.shape[1]
    asked = requests(owner.reshape(1, -1), local_row)
    asked = exchange(asked.reshape(N_ROW, 2, SLOTS), ROW).reshape(2 * N_ROW, SLOTS)
    core = lax.axis_index("core")
    own = dest_feat.T
    part = exchange(answers(asked, features, core.reshape(1)), ROW)
    agg, pre = project(part, own, w_self, w_neigh)
    pair = lax.all_gather(pre.reshape(2, DST // 2, hid), "core", axis=0, tiled=False)
    half = jnp.sum(lax.dynamic_index_in_dim(pair, core, axis=1, keepdims=False, allow_negative_indices=False), axis=0)
    half = half.reshape(3, 8, 4, 256).transpose(0, 2, 1, 3).reshape(N_Z, 8, 256)
    tile = jnp.sum(exchange(half, "z"), axis=0)
    half = exchange(jnp.broadcast_to(tile[None], (N_Z, 8, 256)), "z")
    half = half.reshape(3, 4, 8, 256).transpose(0, 2, 1, 3).reshape(DST // 2, hid)
    pre = lax.all_gather(half, "core", axis=0, tiled=True)
    hidden, part = gradients(pre, grad_out, own, agg)
    total = jnp.sum(exchange(part, ROW), axis=0)
    grads = exchange(jnp.broadcast_to(total[None], (N_ROW, 16, 128)), ROW)
    return (hidden, *spread(grads, hid))


def solution(mesh):
    grid = Mesh(mesh.devices.reshape(8, 4, 12, 2), ("y", "x", "z", "core"))
    return jax.shard_map(
        body,
        mesh=grid,
        in_specs=(P(ROW, COL), P(ROW, COL), P(ROW, None), P(ROW), P(COL, None), P(COL, None), P(ROW, None)),
        out_specs=(P(ROW, None), P(COL, None), P(COL, None)),
        check_vma=False,
    )
```
